512 devices in a mesh: tm: 64 (over x, z, core), row: 8 (over y).
Axes of the slice: x: 4, y: 8, z: 8, core: 2. Of those that a mesh axis runs over, the one named last changes fastest.
Arguments:
- depth_tokens: bfloat16 [512, 8, 16, 768], P('tm', 'row'), may hold values from -6 to 6
- mixer_weight: bfloat16 [768, 800], replicated, may hold values from -0.21875 to 0.21875
- gate_weight: bfloat16 [768, 780], replicated, may hold values from -0.21875 to 0.21875
- conv_kernel: float32 [3, 3, 800], replicated, may hold values from -2 to 2
- conv_bias: float32 [800], replicated, may hold values from -3 to 3
- step_bias: float32 [12], replicated, may hold values from -1 to 1
- decay_rate: float32 [12], replicated, may hold values from 0 to 1, as said below
- skip_gain: float32 [12], replicated, may hold values from 0.5 to 1.5
- norm_gain: float32 [768], replicated, may hold values from 0.1 to 1.9
- out_weight: bfloat16 [768, 768], replicated, may hold values from -0.21875 to 0.21875
Outputs:
- refined: bfloat16 [512, 8, 16, 768], P('tm', 'row')
The draws below stay inside these ranges and needn't reach their ends.
Inputs may be any that keep to these rules, and one draw needn't show every extreme that they name: `decay_rate`: one positive rate per head.
All inputs are finite; a program needn't handle non-finite values.
Results may differ from the reference program's by a relative error of at most 0.0064.
Values may be sent and summed in bfloat16 or wider, within the bound.
A program may use at most 128 MiB of HBM per device.

```python
import jax
import jax.numpy as jnp
from jax import lax

D = 768
HEADS = 12
HEAD_DIM = 64
NSTATE = 16
GW = 16
INNER = 768
CONV_CH = 800
FRAMES = 512
GH = 8


def draw_decay_rate(key, part):
    key = jax.random.fold_in(key, 5)
    spread = jax.random.uniform(key, (HEADS,), jnp.float32)
    lowest = 0.1 / FRAMES
    highest = 0.08
    return jnp.exp(jnp.log(lowest) + spread * (jnp.log(highest) - jnp.log(lowest))).astype(jnp.float32)


def block_levels(key, dims, split, low, largest):
    def one(position, parts):
        draws = jax.random.uniform(jax.random.fold_in(jax.random.fold_in(key, 6), position), (parts,), jnp.float32, low / len(split), largest / len(split))
        return jnp.repeat(jnp.exp(draws), dims[position] // parts).reshape((-1,) + (1,) * (len(dims) - position - 1))

    factor_of = one(*split[0])
    for cut in split[1:]:
        factor_of = factor_of * one(*cut)
    return factor_of


def noise(key, shape, width, reach, split=(), kind=jnp.bfloat16):
    result = width * jax.random.normal(key, shape, jnp.float32)
    if split:
        result = result * block_levels(key, shape, split, -0.22, 0.18)
    return jnp.clip(result, -reach, reach).astype(kind)


def setup_inputs(seed: int = 0) -> dict:
    splits = jax.random.split(jax.random.key(seed), 11)
    return {
        "depth_tokens": noise(splits[0], (FRAMES, GH, GW, D), 1.0, 6.0, ((0, 64), (1, 8))),
        "mixer_weight": noise(splits[1], (D, CONV_CH), D ** -0.5, 0.21875),
        "gate_weight": noise(splits[2], (D, INNER + HEADS), D ** -0.5, 0.21875),
        "conv_kernel": noise(splits[3], (3, 3, CONV_CH), 9 ** -0.5, 2.0, (), jnp.float32),
        "conv_bias": noise(splits[4], (CONV_CH,), 0.5, 3.0, (), jnp.float32),
        "step_bias": jnp.clip(jax.random.uniform(splits[5], (HEADS,), jnp.float32, -1.0, 1.0), -1.0, 1.0),
        "decay_rate": draw_decay_rate(jax.random.fold_in(splits[10], 71), 0),
        "skip_gain": jnp.clip(jax.random.uniform(splits[7], (HEADS,), jnp.float32, 0.5, 1.5), 0.5, 1.5),
        "norm_gain": jnp.clip(1.0 + 0.18 * jax.random.normal(splits[8], (INNER,), jnp.float32), 0.1, 1.9),
        "out_weight": noise(splits[9], (INNER, D), INNER ** -0.5, 0.21875),
    }


def reference(depth_tokens, mixer_weight, gate_weight, conv_kernel, conv_bias, step_bias, decay_rate, skip_gain, norm_gain, out_weight):
    cell_count = GH * GW

    def advance(carry_state, frame_tokens):
        flat_tokens = frame_tokens.reshape(cell_count, D)
        conv_input = jnp.dot(flat_tokens, mixer_weight, preferred_element_type=jnp.float32).astype(jnp.bfloat16)
        gate_step = jnp.dot(flat_tokens, gate_weight, preferred_element_type=jnp.float32).astype(jnp.bfloat16)
        padded = jnp.pad(conv_input.reshape(GH, GW, CONV_CH).astype(jnp.float32), ((1, 1), (1, 1), (0, 0)))
        summed = jnp.zeros((GH, GW, CONV_CH), jnp.float32) + conv_bias
        for row_shift in range(3):
            for col_shift in range(3):
                summed = summed + conv_kernel[row_shift, col_shift] * padded[row_shift:row_shift + GH, col_shift:col_shift + GW]
        activated = jax.nn.silu(summed).reshape(cell_count, CONV_CH)
        values = activated[:, :INNER].reshape(cell_count, HEADS, HEAD_DIM)
        write_keys = activated[:, INNER:INNER + NSTATE]
        read_keys = activated[:, INNER + NSTATE:]
        gate_branch = gate_step[:, :INNER].astype(jnp.float32)
        step_size = jax.nn.softplus(gate_step[:, INNER:].astype(jnp.float32) + step_bias)
        decay = jnp.exp(-step_size * decay_rate)
        carry_state = decay[:, None, :, None] * carry_state + (step_size[:, :, None] * values)[:, None] * write_keys[:, :, None, None]
        mixed = jnp.einsum('cn,cnhp->chp', read_keys, carry_state, precision=lax.Precision.HIGHEST) + skip_gain[None, :, None] * values
        gated_out = mixed.reshape(cell_count, INNER) * jax.nn.silu(gate_branch)
        rms_scale = lax.rsqrt(lax.optimization_barrier(jnp.mean(gated_out * gated_out, axis=-1, keepdims=True)) + 1e-05)
        normed = (gated_out * rms_scale * norm_gain).astype(jnp.bfloat16)
        refined = flat_tokens.astype(jnp.float32) + jnp.dot(normed, out_weight, preferred_element_type=jnp.float32)
        return (carry_state, refined.astype(jnp.bfloat16).reshape(GH, GW, D))
    start_state = jnp.zeros((cell_count, NSTATE, HEADS, HEAD_DIM), jnp.float32)
    final_state, refined = lax.scan(advance, start_state, depth_tokens)
    return refined
```

```python
import functools

import jax
import jax.numpy as jnp
from jax import lax
from jax.experimental import pallas as pl
from jax.experimental.pallas import tpu as pltpu
from jax.sharding import PartitionSpec as P

D = 768
HEADS = 12
GW = 16
INNER = 768
CONV_CH = 800
F = 8
T = F * GW
BLOCKS = 64
CHUNK = 128
EXTRA = 64
STEP = 96

f32 = jnp.float32
bf16 = jnp.bfloat16


def lanes(rows):
    return lax.broadcasted_iota(jnp.int32, (rows, 128), 1)


def dot(a, b, dims=((1,), (0,)), precision=None):
    return lax.dot_general(a, b, (dims, ((), ())), preferred_element_type=f32, precision=precision)


def cell_major():
    r = lax.broadcasted_iota(jnp.int32, (T, T), 0)
    s = lax.broadcasted_iota(jnp.int32, (T, T), 1)
    return jnp.where(s == (r & (F - 1)) * GW + (r >> 3), 1.0, 0.0).astype(bf16)


def frame_major():
    r = lax.broadcasted_iota(jnp.int32, (T, T), 0)
    s = lax.broadcasted_iota(jnp.int32, (T, T), 1)
    return jnp.where(s == (r & (GW - 1)) * F + (r >> 4), 1.0, 0.0).astype(bf16)


def silu(x):
    return x / (1.0 + jnp.exp(-x))


def softplus(x):
    return jnp.maximum(x, 0.0) + jnp.log1p(jnp.exp(-jnp.abs(x)))


def convolve(rows, taps, bias):
    part = []
    for j in range(3):
        part.append(taps[0][j] * rows[0] + taps[1][j] * rows[1] + taps[2][j] * rows[2])
    edge = jnp.zeros((F, rows[0].shape[1]), f32)
    left = jnp.concatenate([edge, part[0][: T - F]], axis=0)
    right = jnp.concatenate([part[2][F:], edge], axis=0)
    return silu(part[1] + left + right + bias)


def second_half(q, tile, keys, steps):
    lane = lanes(T)
    if q % 2:
        tile = pltpu.roll(tile, 64, 1)
    return jnp.where(
        lane < EXTRA,
        tile,
        jnp.where(
            lane < STEP,
            keys,
            jnp.where(
                lane < STEP + 2,
                pltpu.roll(steps, STEP - 2 * q, 1),
                pltpu.roll(steps, STEP + 2 - (8 + q), 1),
            ),
        ),
    )


def packets(first, second):
    n = first.shape[0] // F
    return jnp.concatenate(
        [first.reshape(n, F, 128), second.reshape(n, F, 128)], axis=1
    ).astype(bf16)


def scan_frames(chunks, bias_lane, rate_lane):
    lane = lanes(CHUNK)
    r = lax.broadcasted_iota(jnp.int32, (CHUNK, CHUNK), 0)
    s = lax.broadcasted_iota(jnp.int32, (CHUNK, CHUNK), 1)
    past = s <= r
    tri = jnp.where(past, 1.0, 0.0).astype(f32)
    half = lane < 64
    state1 = jnp.zeros((128, 128), f32)
    state2 = jnp.zeros((128, 128), f32)
    outs = []
    for x1, x2 in chunks:
        step = softplus(x2 + bias_lane)
        cum = dot(tri, -step * rate_lane, precision=lax.Precision.HIGHEST)
        late = jnp.transpose(jnp.log(step) - cum)
        write = jnp.where((lane >= EXTRA) & (lane < EXTRA + 16), x2, 0.0).astype(bf16)
        read = pltpu.roll(x2, 112, 1).astype(bf16)
        pair = dot(read, write, ((1,), (1,)))
        end = cum[CHUNK - 1 :, :]
        weight = jnp.exp(end - cum) * step
        reach = jnp.exp(cum)
        x1b, x2b = x1.astype(bf16), x2.astype(bf16)
        inner = []
        for k, x in enumerate((x1b, x1b, x2b)):
            span = cum[:, STEP + k : STEP + k + 1] + late[STEP + k : STEP + k + 1, :]
            m = pair * jnp.exp(jnp.where(past, span, -1e30))
            inner.append(dot(m.astype(bf16), x))

        def col(a, k):
            return a[:, STEP + k : STEP + k + 1]

        y1 = jnp.where(half, inner[0], inner[1])
        y1 = y1 + jnp.where(half, col(reach, 0), col(reach, 1)) * dot(read, state1.astype(bf16))
        y2 = inner[2] + col(reach, 2) * dot(read, state2.astype(bf16))
        w1 = (x1 * jnp.where(half, col(weight, 0), col(weight, 1))).astype(bf16)
        w2 = (x2 * col(weight, 2)).astype(bf16)
        fade = jnp.exp(end)
        half1 = half[:1]
        state1 = state1 * jnp.where(half1, col(fade, 0), col(fade, 1)) + dot(write, w1, ((0,), (0,)))
        state2 = state2 * col(fade, 2) + dot(write, w2, ((0,), (0,)))
        outs.append((y1, y2))
    return outs


def kernel(
    n_tm,
    n_row,
    tok_hbm,
    mix_hbm,
    gate_hbm,
    out_hbm,
    taps_ref,
    cbias_ref,
    gain_ref,
    sbias_ref,
    rate_ref,
    skip_ref,
    o_ref,
    tok,
    halo,
    mixw,
    gatew,
    outw,
    value,
    gate,
    send1,
    recv1,
    send2,
    recv2,
    load_sem,
    halo_send,
    halo_recv,
    a2a_send,
    a2a_recv,
):
    me = lax.axis_index("tm")
    row = lax.axis_index("row")
    up = lax.rem(row + 1, n_row)
    down = lax.rem(row + n_row - 1, n_row)

    loads = [
        pltpu.make_async_copy(src, dst, load_sem.at[i])
        for i, (src, dst) in enumerate(
            ((tok_hbm, tok), (mix_hbm, mixw), (gate_hbm, gatew), (out_hbm, outw))
        )
    ]
    for load in loads:
        load.start()

    barrier = pltpu.get_barrier_semaphore()
    for other in (up, down):
        pl.semaphore_signal(barrier, inc=1, device_id={"row": other})

    def greet(i, c):
        pl.semaphore_signal(barrier, inc=1, device_id={"tm": lax.rem(me + i, n_tm)})
        return c

    lax.fori_loop(1, n_tm, greet, 0)
    pl.semaphore_wait(barrier, n_tm + 1)

    halos = [
        pltpu.make_async_remote_copy(
            src_ref=tok_hbm,
            dst_ref=halo.at[i],
            send_sem=halo_send.at[i],
            recv_sem=halo_recv.at[i],
            device_id={"row": other},
        )
        for i, other in enumerate((up, down))
    ]
    for copy in halos:
        copy.start()

    perm = cell_major()
    loads[0].wait()
    own = dot(perm, tok[...]).astype(bf16)
    loads[1].wait()
    loads[2].wait()
    gs = dot(own, gatew[...]).astype(bf16).astype(f32)
    gate[...] = gs[:, :INNER]
    steps = jnp.concatenate([gs[:, INNER:], jnp.zeros((T, 128 - HEADS), f32)], axis=1)
    for copy in halos:
        copy.wait()
    low = jnp.where(row > 0, dot(perm, halo[0]), 0.0).astype(bf16)
    high = jnp.where(row < n_row - 1, dot(perm, halo[1]), 0.0).astype(bf16)
    stacked = jnp.concatenate([low, own, high], axis=0)

    def activated(start, size):
        z = dot(stacked, mixw[:, start : start + size]).astype(bf16).astype(f32)
        taps = [[taps_ref[i, j : j + 1, start : start + size] for j in range(3)] for i in range(3)]
        return convolve([z[:T], z[T : 2 * T], z[2 * T :]], taps, cbias_ref[:, start : start + size])

    key = activated(INNER, 32)
    key = jnp.concatenate([key, jnp.zeros((T, 96), f32)], axis=1)
    key = pltpu.roll(key, EXTRA, 1)
    for g in range(3):
        value[:, 256 * g : 256 * (g + 1)] = activated(256 * g, 256)
    for q in range(4):
        tile = value[:, 128 * (4 + q // 2) : 128 * (5 + q // 2)]
        send1[GW * q : GW * (q + 1)] = packets(
            value[:, 128 * q : 128 * (q + 1)], second_half(q, tile, key, steps)
        )

    def exchange(send, recv, which):
        def one(i, c):
            other = lax.rem(me + i, n_tm)
            pltpu.make_async_remote_copy(
                src_ref=send.at[other],
                dst_ref=recv.at[me],
                send_sem=a2a_send.at[which],
                recv_sem=a2a_recv.at[which],
                device_id={"tm": other},
            ).start()
            return c

        lax.fori_loop(1, n_tm, one, 0)
        recv[me] = send[me]
        every = recv.at[pl.ds(0, n_tm - 1)]
        pltpu.make_async_copy(every, every, a2a_recv.at[which]).wait()

    exchange(send1, recv1, 0)

    q = me // GW
    lane = lanes(1)
    bias_lane = jnp.zeros((1, 128), f32)
    rate_lane = jnp.zeros((1, 128), f32)
    for k, head in enumerate((2 * q, 2 * q + 1, 8 + q)):
        bias_lane = jnp.where(lane == STEP + k, sbias_ref[head], bias_lane)
        rate_lane = jnp.where(lane == STEP + k, rate_ref[head], rate_lane)
    chunks = []
    per = CHUNK // F
    for c in range(n_tm // per):
        block = recv1[per * c : per * (c + 1)].astype(f32)
        chunks.append((block[:, :F].reshape(CHUNK, 128), block[:, F:].reshape(CHUNK, 128)))
    for c, (y1, y2) in enumerate(scan_frames(chunks, bias_lane, rate_lane)):
        send2[per * c : per * (c + 1)] = packets(y1, y2)

    exchange(send2, recv2, 1)

    firsts, thirds = [], []
    for q in range(4):
        block = recv2[GW * q : GW * (q + 1)].astype(f32)
        firsts.append(block[:, :F].reshape(T, 128))
        thirds.append(block[:, F:].reshape(T, 128))
    lane = lanes(T)
    for q in (0, 2):
        firsts.append(jnp.where(lane < 64, thirds[q], pltpu.roll(thirds[q + 1], 64, 1)))
    gated = []
    total = jnp.zeros((T, 1), f32)
    for j in range(6):
        cut = slice(128 * j, 128 * (j + 1))
        skip = jnp.where(lane < 64, skip_ref[2 * j], skip_ref[2 * j + 1])
        g = (firsts[j] + skip * value[:, cut]) * silu(gate[:, cut])
        total = total + jnp.sum(g * g, axis=-1, keepdims=True)
        gated.append(g)
    scale = lax.rsqrt(total * (1.0 / INNER) + 1e-5)
    normed = jnp.concatenate(
        [gated[j] * scale * gain_ref[:, 128 * j : 128 * (j + 1)] for j in range(6)], axis=1
    ).astype(bf16)
    normed = dot(frame_major(), normed).astype(bf16)
    loads[3].wait()
    o_ref[...] = (tok[...].astype(f32) + dot(normed, outw[...])).astype(bf16)

    for which, send in ((0, send1), (1, send2)):
        every = send.at[pl.ds(0, n_tm - 1)]
        pltpu.make_async_copy(every, every, a2a_send.at[which]).wait()


def per_device(
    n_tm,
    n_row,
    depth_tokens,
    mixer_weight,
    gate_weight,
    conv_kernel,
    conv_bias,
    step_bias,
    decay_rate,
    skip_gain,
    norm_gain,
    out_weight,
):
    hbm = pl.BlockSpec(memory_space=pl.ANY)
    vmem = pl.BlockSpec(memory_space=pltpu.VMEM)
    smem = pl.BlockSpec(memory_space=pltpu.SMEM)
    out = pl.pallas_call(
        functools.partial(kernel, n_tm, n_row),
        out_shape=jax.ShapeDtypeStruct((T, D), bf16),
        in_specs=[hbm] * 4 + [vmem] * 3 + [smem] * 3,
        out_specs=vmem,
        scratch_shapes=[
            pltpu.VMEM((T, D), bf16),
            pltpu.VMEM((2, T, D), bf16),
            pltpu.VMEM((D, CONV_CH), bf16),
            pltpu.VMEM((D, INNER + HEADS), bf16),
            pltpu.VMEM((INNER, D), bf16),
            pltpu.VMEM((T, INNER), f32),
            pltpu.VMEM((T, INNER), f32),
            pltpu.VMEM((BLOCKS, 2 * F, 128), bf16),
            pltpu.VMEM((BLOCKS, 2 * F, 128), bf16),
            pltpu.VMEM((BLOCKS, 2 * F, 128), bf16),
            pltpu.VMEM((BLOCKS, 2 * F, 128), bf16),
            pltpu.SemaphoreType.DMA((4,)),
            pltpu.SemaphoreType.DMA((2,)),
            pltpu.SemaphoreType.DMA((2,)),
            pltpu.SemaphoreType.DMA((2,)),
            pltpu.SemaphoreType.DMA((2,)),
        ],
        compiler_params=pltpu.CompilerParams(
            collective_id=0, has_side_effects=True, vmem_limit_bytes=48 * 1024 * 1024
        ),
    )(
        depth_tokens.reshape(T, D),
        mixer_weight,
        gate_weight,
        out_weight,
        conv_kernel,
        conv_bias.reshape(1, CONV_CH),
        norm_gain.reshape(1, INNER),
        step_bias,
        decay_rate,
        skip_gain,
    )
    return out.reshape(depth_tokens.shape)


def solution(mesh):
    placed = (P("tm", "row", None, None), P(), P(), P(), P(), P(), P(), P(), P(), P())
    return jax.shard_map(
        functools.partial(per_device, mesh.shape["tm"], mesh.shape["row"]),
        mesh=mesh,
        in_specs=placed,
        out_specs=P("tm", "row", None, None),
        check_vma=False,
    )
```

```python
import functools

import jax
import jax.numpy as jnp
from jax import lax
from jax.experimental import pallas as pl
from jax.experimental.pallas import tpu as pltpu
from jax.sharding import PartitionSpec as P

D = 768
HEADS = 12
NSTATE = 16
GW = 16
INNER = 768
CONV_CH = 800
F = 8
T = F * GW
GROUP = 16
SPAN = 128
KEY = 0
STEP = 32

NT = ((1,), (1,))
TN = ((0,), (0,))
f32 = jnp.float32
bf16 = jnp.bfloat16


def lanes(rows):
    return lax.broadcasted_iota(jnp.int32, (rows, 128), 1)


def dot(a, b, dims=((1,), (0,)), precision=None):
    return lax.dot_general(a, b, (dims, ((), ())), preferred_element_type=f32, precision=precision)


def cell_major():
    r = lax.broadcasted_iota(jnp.int32, (T, T), 0)
    s = lax.broadcasted_iota(jnp.int32, (T, T), 1)
    return jnp.where(s == (r & (F - 1)) * GW + (r >> 3), 1.0, 0.0).astype(bf16)


def frame_major():
    r = lax.broadcasted_iota(jnp.int32, (T, T), 0)
    s = lax.broadcasted_iota(jnp.int32, (T, T), 1)
    return jnp.where(s == (r & (GW - 1)) * F + (r >> 4), 1.0, 0.0).astype(bf16)


def silu(x):
    return x / (1.0 + jnp.exp(-x))


def softplus(x):
    return jnp.maximum(x, 0.0) + jnp.log1p(jnp.exp(-jnp.abs(x)))


def convolve(rows, taps, bias):
    part = []
    for j in range(3):
        part.append(taps[0][j] * rows[0] + taps[1][j] * rows[1] + taps[2][j] * rows[2])
    edge = jnp.zeros((F, rows[0].shape[1]), f32)
    left = jnp.concatenate([edge, part[0][: T - F]], axis=0)
    right = jnp.concatenate([part[2][F:], edge], axis=0)
    return silu(part[1] + left + right + bias)


def packets(tiles):
    return jnp.concatenate([t.reshape(GW, F, 128) for t in tiles], axis=1).astype(bf16)


def unpack(block, j):
    return block[:, F * j : F * (j + 1)].reshape(SPAN, 128)


def kernel(
    n_tm,
    n_row,
    tok_hbm,
    mix_hbm,
    gate_hbm,
    out_hbm,
    taps_hbm,
    cbias_hbm,
    gain_hbm,
    sbias_ref,
    rate_ref,
    skip_ref,
    o_ref,
    tok,
    halo,
    mixw,
    gatew,
    outw,
    taps_ref,
    cbias_ref,
    gain_ref,
    center,
    value,
    gate,
    send1,
    recv1,
    state_out,
    state_in,
    fade_out,
    fade_in,
    send2,
    recv2,
    load_sem,
    halo_send,
    halo_recv,
    one_send,
    one_recv,
    state_send,
    state_recv,
    two_send,
    two_recv,
):
    me = lax.axis_index("tm")
    row = lax.axis_index("row")
    up = lax.rem(row + 1, n_row)
    down = lax.rem(row + n_row - 1, n_row)
    n_groups = n_tm // GROUP
    group = me // GROUP
    member = lax.rem(me, GROUP)

    def peer(i):
        return lax.rem(member + i, GROUP)

    barrier = pltpu.get_barrier_semaphore()
    for other in (up, down):
        pl.semaphore_signal(barrier, inc=1, device_id={"row": other})

    def greet(i, c):
        pl.semaphore_signal(barrier, inc=1, device_id={"tm": group * GROUP + peer(i)})
        return c

    lax.fori_loop(1, GROUP, greet, 0)
    for i in range(1, n_groups):
        pl.semaphore_signal(barrier, inc=1, device_id={"tm": lax.rem(me + GROUP * i, n_tm)})

    loads = [
        pltpu.make_async_copy(src, dst, load_sem.at[i])
        for i, (src, dst) in enumerate(
            (
                (tok_hbm, tok),
                (gate_hbm, gatew),
                (mix_hbm, mixw),
                (taps_hbm, taps_ref),
                (cbias_hbm, cbias_ref),
                (gain_hbm, gain_ref),
                (out_hbm, outw),
            )
        )
    ]
    for load in loads:
        load.start()
    pl.semaphore_wait(barrier, 2 + GROUP - 1 + n_groups - 1)

    halos = [
        pltpu.make_async_remote_copy(
            src_ref=tok_hbm,
            dst_ref=halo.at[i],
            send_sem=halo_send.at[i],
            recv_sem=halo_recv.at[i],
            device_id={"row": other},
        )
        for i, other in enumerate((up, down))
    ]
    for copy in halos:
        copy.start()

    perm = cell_major()
    loads[0].wait()
    own = dot(perm, tok[...]).astype(bf16)
    loads[1].wait()
    gs = dot(own, gatew[...], NT).astype(bf16).astype(f32)
    gate[...] = gs[:, :INNER]
    steps = jnp.concatenate([gs[:, INNER:], jnp.zeros((T, 128 - HEADS), f32)], axis=1)
    steps = pltpu.roll(steps, STEP, 1)
    loads[2].wait()
    center[...] = dot(own, mixw[...], NT).astype(bf16).astype(f32)
    for load in loads[3:5]:
        load.wait()

    for copy in halos:
        copy.wait()
    low = jnp.where(row > 0, dot(perm, halo[0]), 0.0).astype(bf16)
    high = jnp.where(row < n_row - 1, dot(perm, halo[1]), 0.0).astype(bf16)
    sides = jnp.concatenate([low, high], axis=0)

    def activated(start, size):
        z = dot(sides, mixw[start : start + size, :], NT).astype(bf16).astype(f32)
        taps = [[taps_ref[i, j : j + 1, start : start + size] for j in range(3)] for i in range(3)]
        rows = [z[:T], center[:, start : start + size], z[T:]]
        return convolve(rows, taps, cbias_ref[start : start + size].reshape(1, size))

    def send_all(send, recv, send_sem, recv_sem):
        def one(i, c):
            other = peer(i)
            pltpu.make_async_remote_copy(
                src_ref=send.at[other],
                dst_ref=recv.at[member],
                send_sem=send_sem,
                recv_sem=recv_sem,
                device_id={"tm": group * GROUP + other},
            ).start()
            return c

        lax.fori_loop(1, GROUP, one, 0)
        recv[member] = send[member]

    def wait_all(buf, sem, count=GROUP - 1):
        every = buf.at[pl.ds(0, count)]
        pltpu.make_async_copy(every, every, sem).wait()

    key = activated(INNER, 32)
    key = jnp.concatenate([key, jnp.zeros((T, 96), f32)], axis=1)
    extra = jnp.where(lanes(T) < STEP, key, steps)
    first = activated(0, 384)
    value[:, :384] = first
    send1[0] = packets([extra] + [first[:, 128 * j : 128 * (j + 1)] for j in range(3)])
    send_all(send1.at[0], recv1.at[0], one_send.at[0], one_recv.at[0])
    second = activated(384, 384)
    value[:, 384:] = second
    send1[1] = packets(
        [second[:, 128 * j : 128 * (j + 1)] for j in range(3)] + [jnp.zeros((T, 128), f32)]
    )
    send_all(send1.at[1], recv1.at[1], one_send.at[1], one_recv.at[1])

    lane = lanes(1)
    bias_lane = jnp.zeros((1, 128), f32)
    rate_lane = jnp.zeros((1, 128), f32)
    for h in range(HEADS):
        bias_lane = jnp.where(lane == STEP + h, sbias_ref[h], bias_lane)
        rate_lane = jnp.where(lane == STEP + h, rate_ref[h], rate_lane)
    r = lax.broadcasted_iota(jnp.int32, (SPAN, SPAN), 0)
    s = lax.broadcasted_iota(jnp.int32, (SPAN, SPAN), 1)
    past = s <= r
    half = lanes(SPAN) < 64

    def col(a, h):
        return a[:, STEP + h : STEP + h + 1]

    def both(a, j):
        return jnp.where(half[: a.shape[0]], col(a, 2 * j), col(a, 2 * j + 1))

    def send_state(part):
        for i in range(1, n_groups):
            pltpu.make_async_remote_copy(
                src_ref=state_out.at[part],
                dst_ref=state_in.at[part, i - 1],
                send_sem=state_send.at[part],
                recv_sem=state_recv.at[part],
                device_id={"tm": lax.rem(me + GROUP * i, n_tm)},
            ).start()

    wait_all(recv1.at[0], one_recv.at[0])
    block = recv1[0].astype(f32)
    extra = unpack(block, 0)
    x = [unpack(block, j) for j in range(1, 4)]
    step = softplus(extra + bias_lane)
    tri = jnp.where(past, 1.0, 0.0).astype(f32)
    cum = dot(tri, -step * rate_lane, precision=lax.Precision.HIGHEST)
    end = cum[SPAN - 1 :, :]
    fade_out[...] = jnp.broadcast_to(end, (8, 128))
    for i in range(1, n_groups):
        pltpu.make_async_remote_copy(
            src_ref=fade_out,
            dst_ref=fade_in.at[i - 1],
            send_sem=state_send.at[2],
            recv_sem=state_recv.at[2],
            device_id={"tm": lax.rem(me + GROUP * i, n_tm)},
        ).start()
    weight = jnp.exp(end - cum) * step
    write = extra[:, :NSTATE].astype(bf16)
    read = extra[:, NSTATE : 2 * NSTATE].astype(bf16)
    scaled = jnp.concatenate([x[j] * both(weight, j) for j in range(3)], axis=1).astype(bf16)
    state_out[0] = dot(write, scaled, TN).astype(bf16)
    send_state(0)
    wait_all(recv1.at[1], one_recv.at[1])
    block = recv1[1].astype(f32)
    x = x + [unpack(block, j) for j in range(3)]
    scaled = jnp.concatenate([x[j] * both(weight, j) for j in range(3, 6)], axis=1).astype(bf16)
    state_out[1] = dot(write, scaled, TN).astype(bf16)
    send_state(1)

    late = jnp.transpose(jnp.log(step) - cum)
    reach = jnp.exp(cum)
    pair = dot(read, write, NT)
    inner = []
    for j in range(6):
        xb = x[j].astype(bf16)
        part = []
        for h in (2 * j, 2 * j + 1):
            span = col(cum, h) + late[STEP + h : STEP + h + 1, :]
            m = pair * jnp.exp(jnp.where(past, span, -1e30))
            part.append(dot(m.astype(bf16), xb))
        inner.append(jnp.where(half, part[0], part[1]))

    wait_all(fade_in, state_recv.at[2], n_groups - 1)
    fades = [jnp.exp(fade_in[i][:1]) for i in range(n_groups - 1)]

    def arrived(part):
        wait_all(state_in.at[part], state_recv.at[part], n_groups - 1)
        total = jnp.zeros((NSTATE, 384), f32)
        for i in range(n_groups - 2, -1, -1):
            fade = jnp.concatenate([both(fades[i], 3 * part + j) for j in range(3)], axis=1)
            total = jnp.where(group > i, total * fade + state_in[part, i].astype(f32), 0.0)
        return dot(read, total.astype(bf16))

    def send_back(third, tiles):
        send2[third] = packets(tiles)
        send_all(send2.at[third], recv2.at[third], two_send.at[third], two_recv.at[third])

    def result(carried, j):
        k = j % 3
        return inner[j] + both(reach, j) * carried[:, 128 * k : 128 * (k + 1)]

    carried = arrived(0)
    send_back(0, [result(carried, 0), result(carried, 1)])
    third = result(carried, 2)
    carried = arrived(1)
    send_back(1, [third, result(carried, 3)])
    send_back(2, [result(carried, 4), result(carried, 5)])

    loads[5].wait()
    lane = lanes(1)
    gated = []
    total = jnp.zeros((T, 1), f32)
    for third in range(3):
        wait_all(recv2.at[third], two_recv.at[third])
        block = recv2[third].astype(f32)
        for k in range(2):
            j = 2 * third + k
            cut = slice(128 * j, 128 * (j + 1))
            skip = jnp.where(lane < 64, skip_ref[2 * j], skip_ref[2 * j + 1])
            g = (unpack(block, k) + skip * value[:, cut]) * silu(gate[:, cut])
            total = total + jnp.sum(g * g, axis=-1, keepdims=True)
            gated.append(g * gain_ref[cut].reshape(1, 128))
    scale = lax.rsqrt(total * (1.0 / INNER) + 1e-5)
    normed = jnp.concatenate([g * scale for g in gated], axis=1).astype(bf16)
    normed = dot(frame_major(), normed).astype(bf16)
    loads[6].wait()
    o_ref[...] = (tok[...].astype(f32) + dot(normed, outw[...])).astype(bf16)

    for part in range(2):
        wait_all(send1.at[part], one_send.at[part])
        wait_all(state_in.at[part], state_send.at[part], n_groups - 1)
    wait_all(fade_in, state_send.at[2], n_groups - 1)
    for third in range(3):
        wait_all(send2.at[third], two_send.at[third])


def per_device(
    n_tm,
    n_row,
    depth_tokens,
    mixer_weight,
    gate_weight,
    conv_kernel,
    conv_bias,
    step_bias,
    decay_rate,
    skip_gain,
    norm_gain,
    out_weight,
):
    hbm = pl.BlockSpec(memory_space=pl.ANY)
    vmem = pl.BlockSpec(memory_space=pltpu.VMEM)
    smem = pl.BlockSpec(memory_space=pltpu.SMEM)
    dma = pltpu.SemaphoreType.DMA
    n_groups = n_tm // GROUP
    out = pl.pallas_call(
        functools.partial(kernel, n_tm, n_row),
        out_shape=jax.ShapeDtypeStruct((T, D), bf16),
        in_specs=[hbm] * 7 + [smem] * 3,
        out_specs=vmem,
        scratch_shapes=[
            pltpu.VMEM((T, D), bf16),
            pltpu.VMEM((2, T, D), bf16),
            pltpu.VMEM((CONV_CH, D), bf16),
            pltpu.VMEM((INNER + HEADS, D), bf16),
            pltpu.VMEM((INNER, D), bf16),
            pltpu.VMEM((3, 3, CONV_CH), f32),
            pltpu.VMEM((CONV_CH,), f32),
            pltpu.VMEM((INNER,), f32),
            pltpu.VMEM((T, CONV_CH), f32),
            pltpu.VMEM((T, INNER), f32),
            pltpu.VMEM((T, INNER), f32),
            pltpu.VMEM((2, GROUP, 4 * F, 128), bf16),
            pltpu.VMEM((2, GROUP, 4 * F, 128), bf16),
            pltpu.VMEM((2, NSTATE, 384), bf16),
            pltpu.VMEM((2, n_groups - 1, NSTATE, 384), bf16),
            pltpu.VMEM((8, 128), f32),
            pltpu.VMEM((n_groups - 1, 8, 128), f32),
            pltpu.VMEM((3, GROUP, 2 * F, 128), bf16),
            pltpu.VMEM((3, GROUP, 2 * F, 128), bf16),
            dma((7,)),
            dma((2,)),
            dma((2,)),
            dma((2,)),
            dma((2,)),
            dma((3,)),
            dma((3,)),
            dma((3,)),
            dma((3,)),
        ],
        compiler_params=pltpu.CompilerParams(
            collective_id=0, has_side_effects=True, vmem_limit_bytes=60 * 1024 * 1024
        ),
    )(
        depth_tokens.reshape(T, D),
        mixer_weight.T,
        gate_weight.T,
        out_weight,
        conv_kernel,
        conv_bias,
        norm_gain,
        step_bias,
        decay_rate,
        skip_gain,
    )
    return out.reshape(depth_tokens.shape)


def solution(mesh):
    placed = (P("tm", "row", None, None), P(), P(), P(), P(), P(), P(), P(), P(), P())
    return jax.shard_map(
        functools.partial(per_device, mesh.shape["tm"], mesh.shape["row"]),
        mesh=mesh,
        in_specs=placed,
        out_specs=P("tm", "row", None, None),
        check_vma=False,
    )
```

```python
import functools

import jax
import jax.numpy as jnp
from jax import lax
from jax.experimental import pallas as pl
from jax.experimental.pallas import tpu as pltpu
from jax.sharding import PartitionSpec as P

D = 768
HEADS = 12
NSTATE = 16
GW = 16
INNER = 768
CONV_CH = 800
F = 8
T = F * GW
GROUP = 16
SPAN = 128
HALF = 64
PIECE = 80
KEY = 0
STEP = 32

NT = ((1,), (1,))
TN = ((0,), (0,))
f32 = jnp.float32
bf16 = jnp.bfloat16


def lanes(rows):
    return lax.broadcasted_iota(jnp.int32, (rows, 128), 1)


def dot(a, b, dims=((1,), (0,)), precision=None):
    return lax.dot_general(a, b, (dims, ((), ())), preferred_element_type=f32, precision=precision)


def cell_major():
    r = lax.broadcasted_iota(jnp.int32, (T, T), 0)
    s = lax.broadcasted_iota(jnp.int32, (T, T), 1)
    return jnp.where(s == (r & (F - 1)) * GW + (r >> 3), 1.0, 0.0).astype(bf16)


def frame_major():
    r = lax.broadcasted_iota(jnp.int32, (T, T), 0)
    s = lax.broadcasted_iota(jnp.int32, (T, T), 1)
    return jnp.where(s == (r & (GW - 1)) * F + (r >> 4), 1.0, 0.0).astype(bf16)


def silu(x):
    return x / (1.0 + jnp.exp(-x))


def softplus(x):
    return jnp.maximum(x, 0.0) + jnp.log1p(jnp.exp(-jnp.abs(x)))


def convolve(wave, rows, taps, bias):
    low, high = HALF * wave, HALF * (wave + 1)

    def part(j, start, stop):
        z = [r(start, stop) for r in rows]
        return taps[0][j] * z[0] + taps[1][j] * z[1] + taps[2][j] * z[2]

    edge = jnp.zeros((F, bias.shape[1]), f32)
    if wave == 0:
        left = jnp.concatenate([edge, part(0, low, high - F)], axis=0)
        right = part(2, low + F, high + F)
    else:
        left = part(0, low - F, high - F)
        right = jnp.concatenate([part(2, low + F, high), edge], axis=0)
    return silu(part(1, low, high) + left + right + bias)


def packets(tiles):
    return jnp.concatenate([t.reshape(-1, F, 128) for t in tiles], axis=1).astype(bf16)


def unpack(block, j):
    return block[:, F * j : F * (j + 1)].reshape(SPAN, 128)


def kernel(
    n_tm,
    n_row,
    tok_hbm,
    mix_hbm,
    gate_hbm,
    out_hbm,
    taps_hbm,
    cbias_hbm,
    gain_hbm,
    sbias_ref,
    rate_ref,
    skip_ref,
    o_ref,
    tok,
    halo,
    mixw,
    gatew,
    outw,
    taps_ref,
    cbias_ref,
    gain_ref,
    mine,
    center,
    side,
    value,
    gate,
    send1,
    recv1,
    state_out,
    state_in,
    fade_out,
    fade_in,
    send2,
    recv2,
    load_sem,
    halo_send,
    halo_recv,
    one_send,
    one_recv,
    state_send,
    state_recv,
    two_send,
    two_recv,
):
    me = lax.axis_index("tm")
    row = lax.axis_index("row")
    up = lax.rem(row + 1, n_row)
    down = lax.rem(row + n_row - 1, n_row)
    n_groups = n_tm // GROUP
    group = me // GROUP
    member = lax.rem(me, GROUP)
    chip = member // 2
    core = lax.rem(member, 2)
    cell = core * (GW // 2) + chip

    def peer(i):
        return lax.rem(member + i, GROUP)

    barrier = pltpu.get_barrier_semaphore()
    for other in (up, down):
        pl.semaphore_signal(barrier, inc=1, device_id={"row": other})

    def greet(i, c):
        pl.semaphore_signal(barrier, inc=1, device_id={"tm": group * GROUP + peer(i)})
        return c

    lax.fori_loop(1, GROUP, greet, 0)
    for i in range(1, n_groups):
        pl.semaphore_signal(barrier, inc=1, device_id={"tm": lax.rem(me + GROUP * i, n_tm)})

    loads = [
        pltpu.make_async_copy(src, dst, load_sem.at[i])
        for i, (src, dst) in enumerate(
            (
                (tok_hbm, tok),
                (gate_hbm, gatew),
                (mix_hbm, mixw),
                (taps_hbm, taps_ref),
                (cbias_hbm, cbias_ref),
                (gain_hbm, gain_ref),
                (out_hbm, outw),
            )
        )
    ]
    for load in loads:
        load.start()
    perm = cell_major()
    loads[0].wait()
    own = dot(perm, tok[...]).astype(bf16)
    mine[...] = own
    pl.semaphore_wait(barrier, 2 + GROUP - 1 + n_groups - 1)

    pieces = (pl.ds(0, PIECE), pl.ds(PIECE, T - PIECE))
    halos = [
        [
            pltpu.make_async_remote_copy(
                src_ref=mine.at[piece],
                dst_ref=halo.at[i, piece],
                send_sem=halo_send.at[i, w],
                recv_sem=halo_recv.at[i, w],
                device_id={"row": other},
            )
            for i, other in enumerate((up, down))
        ]
        for w, piece in enumerate(pieces)
    ]
    for copy in halos[0] + halos[1]:
        copy.start()

    loads[1].wait()
    gs = dot(own, gatew[...], NT).astype(bf16).astype(f32)
    gate[...] = gs[:, :INNER]
    steps = jnp.concatenate([gs[:, INNER:], jnp.zeros((T, 128 - HEADS), f32)], axis=1)
    steps = pltpu.roll(steps, STEP, 1)
    loads[2].wait()
    center[...] = dot(own, mixw[...], NT).astype(bf16).astype(f32)
    for load in loads[3:5]:
        load.wait()

    def activated(wave, sides, start, size):
        z = dot(sides, mixw[start : start + size, :], NT).astype(bf16).astype(f32)
        n = z.shape[0] // 2
        cols = slice(start, start + size)
        new = slice(0, PIECE) if wave == 0 else slice(PIECE, T)
        side[0, new, cols] = jnp.where(row > 0, z[:n], 0.0)
        side[1, new, cols] = jnp.where(row < n_row - 1, z[n:], 0.0)
        taps = [[taps_ref[i, j : j + 1, cols] for j in range(3)] for i in range(3)]
        rows = [
            lambda a, b: side[0, a:b, cols],
            lambda a, b: center[a:b, cols],
            lambda a, b: side[1, a:b, cols],
        ]
        return convolve(wave, rows, taps, cbias_ref[cols].reshape(1, size))

    def send_wave(wave, part):
        def copy(other):
            return pltpu.make_async_remote_copy(
                src_ref=send1.at[part, GW // 2 * wave + other],
                dst_ref=recv1.at[part, member],
                send_sem=one_send.at[part],
                recv_sem=one_recv.at[part],
                device_id={"tm": group * GROUP + 2 * other + wave},
            )

        def one(i, c):
            copy(lax.rem(chip + i, GROUP // 2)).start()
            return c

        lax.fori_loop(1, GROUP // 2, one, 0)

        @pl.when(core == wave)
        def _():
            recv1[part, member] = send1[part, cell]

        @pl.when(core != wave)
        def _():
            copy(chip).start()

    def return_all(send, recv, send_sem, recv_sem):
        def one(i, c):
            other = peer(i)
            pltpu.make_async_remote_copy(
                src_ref=send.at[other],
                dst_ref=recv.at[cell],
                send_sem=send_sem,
                recv_sem=recv_sem,
                device_id={"tm": group * GROUP + other},
            ).start()
            return c

        lax.fori_loop(1, GROUP, one, 0)
        recv[cell] = send[member]

    def wait_all(buf, sem, count=GROUP - 1):
        every = buf.at[pl.ds(0, count)]
        pltpu.make_async_copy(every, every, sem).wait()

    for wave in range(2):
        for copy in halos[wave]:
            copy.wait_recv()
        rows = slice(HALF * wave, HALF * (wave + 1))
        cells = slice(GW // 2 * wave, GW // 2 * (wave + 1))
        sides = halo[:, :PIECE] if wave == 0 else halo[:, PIECE:]
        sides = sides.reshape(-1, D)
        key = activated(wave, sides, INNER, 32)
        key = jnp.concatenate([key, jnp.zeros((HALF, 96), f32)], axis=1)
        extra = jnp.where(lanes(HALF) < STEP, key, steps[rows])
        act = activated(wave, sides, 0, 384)
        value[rows, :384] = act
        send1[0, cells] = packets([extra] + [act[:, 128 * j : 128 * (j + 1)] for j in range(3)])
        send_wave(wave, 0)
        act = activated(wave, sides, 384, 384)
        value[rows, 384:] = act
        send1[1, cells] = packets(
            [act[:, 128 * j : 128 * (j + 1)] for j in range(3)] + [jnp.zeros((HALF, 128), f32)]
        )
        send_wave(wave, 1)

    lane = lanes(1)
    bias_lane = jnp.zeros((1, 128), f32)
    rate_lane = jnp.zeros((1, 128), f32)
    for h in range(HEADS):
        bias_lane = jnp.where(lane == STEP + h, sbias_ref[h], bias_lane)
        rate_lane = jnp.where(lane == STEP + h, rate_ref[h], rate_lane)
    r = lax.broadcasted_iota(jnp.int32, (SPAN, SPAN), 0)
    s = lax.broadcasted_iota(jnp.int32, (SPAN, SPAN), 1)
    past = s <= r
    half = lanes(SPAN) < 64

    def col(a, h):
        return a[:, STEP + h : STEP + h + 1]

    def both(a, j):
        return jnp.where(half[: a.shape[0]], col(a, 2 * j), col(a, 2 * j + 1))

    def send_state(part):
        for i in range(1, n_groups):
            pltpu.make_async_remote_copy(
                src_ref=state_out.at[part],
                dst_ref=state_in.at[part, i - 1],
                send_sem=state_send.at[part],
                recv_sem=state_recv.at[part],
                device_id={"tm": lax.rem(me + GROUP * i, n_tm)},
            ).start()

    wait_all(recv1.at[0], one_recv.at[0])
    block = recv1[0].astype(f32)
    extra = unpack(block, 0)
    x = [unpack(block, j) for j in range(1, 4)]
    step = softplus(extra + bias_lane)
    tri = jnp.where(past, 1.0, 0.0).astype(f32)
    cum = dot(tri, -step * rate_lane, precision=lax.Precision.HIGHEST)
    end = cum[SPAN - 1 :, :]
    fade_out[...] = jnp.broadcast_to(end, (8, 128))
    for i in range(1, n_groups):
        pltpu.make_async_remote_copy(
            src_ref=fade_out,
            dst_ref=fade_in.at[i - 1],
            send_sem=state_send.at[2],
            recv_sem=state_recv.at[2],
            device_id={"tm": lax.rem(me + GROUP * i, n_tm)},
        ).start()
    weight = jnp.exp(end - cum) * step
    write = extra[:, :NSTATE].astype(bf16)
    read = extra[:, NSTATE : 2 * NSTATE].astype(bf16)
    scaled = jnp.concatenate([x[j] * both(weight, j) for j in range(3)], axis=1).astype(bf16)
    state_out[0] = dot(write, scaled, TN).astype(bf16)
    send_state(0)
    wait_all(recv1.at[1], one_recv.at[1])
    block = recv1[1].astype(f32)
    x = x + [unpack(block, j) for j in range(3)]
    scaled = jnp.concatenate([x[j] * both(weight, j) for j in range(3, 6)], axis=1).astype(bf16)
    state_out[1] = dot(write, scaled, TN).astype(bf16)
    send_state(1)

    late = jnp.transpose(jnp.log(step) - cum)
    reach = jnp.exp(cum)
    pair = dot(read, write, NT)
    inner = []
    for j in range(6):
        xb = x[j].astype(bf16)
        part = []
        for h in (2 * j, 2 * j + 1):
            span = col(cum, h) + late[STEP + h : STEP + h + 1, :]
            m = pair * jnp.exp(jnp.where(past, span, -1e30))
            part.append(dot(m.astype(bf16), xb))
        inner.append(jnp.where(half, part[0], part[1]))

    wait_all(fade_in, state_recv.at[2], n_groups - 1)
    fades = [jnp.exp(fade_in[i][:1]) for i in range(n_groups - 1)]

    def arrived(part):
        wait_all(state_in.at[part], state_recv.at[part], n_groups - 1)
        total = jnp.zeros((NSTATE, 384), f32)
        for i in range(n_groups - 2, -1, -1):
            fade = jnp.concatenate([both(fades[i], 3 * part + j) for j in range(3)], axis=1)
            total = jnp.where(group > i, total * fade + state_in[part, i].astype(f32), 0.0)
        return dot(read, total.astype(bf16))

    def send_back(third, tiles):
        send2[third] = packets(tiles)
        return_all(send2.at[third], recv2.at[third], two_send.at[third], two_recv.at[third])

    def result(carried, j):
        k = j % 3
        return inner[j] + both(reach, j) * carried[:, 128 * k : 128 * (k + 1)]

    carried = arrived(0)
    send_back(0, [result(carried, 0), result(carried, 1)])
    third = result(carried, 2)
    carried = arrived(1)
    send_back(1, [third, result(carried, 3)])
    send_back(2, [result(carried, 4), result(carried, 5)])

    loads[5].wait()
    lane = lanes(1)
    gated = []
    total = jnp.zeros((T, 1), f32)
    for third in range(3):
        wait_all(recv2.at[third], two_recv.at[third])
        block = recv2[third].astype(f32)
        for k in range(2):
            j = 2 * third + k
            cut = slice(128 * j, 128 * (j + 1))
            skip = jnp.where(lane < 64, skip_ref[2 * j], skip_ref[2 * j + 1])
            g = (unpack(block, k) + skip * value[:, cut]) * silu(gate[:, cut])
            total = total + jnp.sum(g * g, axis=-1, keepdims=True)
            gated.append(g * gain_ref[cut].reshape(1, 128))
    scale = lax.rsqrt(total * (1.0 / INNER) + 1e-5)
    normed = jnp.concatenate([g * scale for g in gated], axis=1).astype(bf16)
    normed = dot(frame_major(), normed).astype(bf16)
    loads[6].wait()
    o_ref[...] = (tok[...].astype(f32) + dot(normed, outw[...])).astype(bf16)

    for copy in halos[0] + halos[1]:
        copy.wait_send()
    for part in range(2):
        wait_all(send1.at[part], one_send.at[part])
        wait_all(state_in.at[part], state_send.at[part], n_groups - 1)
    wait_all(fade_in, state_send.at[2], n_groups - 1)
    for third in range(3):
        wait_all(send2.at[third], two_send.at[third])


def per_device(
    n_tm,
    n_row,
    depth_tokens,
    mixer_weight,
    gate_weight,
    conv_kernel,
    conv_bias,
    step_bias,
    decay_rate,
    skip_gain,
    norm_gain,
    out_weight,
):
    hbm = pl.BlockSpec(memory_space=pltpu.HBM)
    vmem = pl.BlockSpec(memory_space=pltpu.VMEM)
    smem = pl.BlockSpec(memory_space=pltpu.SMEM)
    dma = pltpu.SemaphoreType.DMA
    n_groups = n_tm // GROUP
    out = pl.pallas_call(
        functools.partial(kernel, n_tm, n_row),
        out_shape=pltpu.VMEM((T, D), bf16),
        in_specs=[hbm] * 7 + [smem] * 3,
        out_specs=vmem,
        scratch_shapes=[
            pltpu.VMEM((T, D), bf16),
            pltpu.VMEM((2, T, D), bf16),
            pltpu.VMEM((CONV_CH, D), bf16),
            pltpu.VMEM((INNER + HEADS, D), bf16),
            pltpu.VMEM((INNER, D), bf16),
            pltpu.VMEM((3, 3, CONV_CH), f32),
            pltpu.VMEM((CONV_CH,), f32),
            pltpu.VMEM((INNER,), f32),
            pltpu.VMEM((T, D), bf16),
            pltpu.VMEM((T, CONV_CH), f32),
            pltpu.VMEM((2, T, CONV_CH), f32),
            pltpu.VMEM((T, INNER), f32),
            pltpu.VMEM((T, INNER), f32),
            pltpu.VMEM((2, GROUP, 4 * F, 128), bf16),
            pltpu.VMEM((2, GROUP, 4 * F, 128), bf16),
            pltpu.VMEM((2, NSTATE, 384), bf16),
            pltpu.VMEM((2, n_groups - 1, NSTATE, 384), bf16),
            pltpu.VMEM((8, 128), f32),
            pltpu.VMEM((n_groups - 1, 8, 128), f32),
            pltpu.VMEM((3, GROUP, 2 * F, 128), bf16),
            pltpu.VMEM((3, GROUP, 2 * F, 128), bf16),
            dma((7,)),
            dma((2, 2)),
            dma((2, 2)),
            dma((2,)),
            dma((2,)),
            dma((3,)),
            dma((3,)),
            dma((3,)),
            dma((3,)),
        ],
        compiler_params=pltpu.CompilerParams(
            collective_id=0, has_side_effects=True, vmem_limit_bytes=56 * 1024 * 1024
        ),
    )(
        depth_tokens.reshape(T, D),
        mixer_weight.T,
        gate_weight.T,
        out_weight,
        conv_kernel,
        conv_bias,
        norm_gain,
        step_bias,
        decay_rate,
        skip_gain,
    )
    return out.reshape(depth_tokens.shape)


def solution(mesh):
    placed = (P("tm", "row", None, None), P(), P(), P(), P(), P(), P(), P(), P(), P())
    return jax.shard_map(
        functools.partial(per_device, mesh.shape["tm"], mesh.shape["row"]),
        mesh=mesh,
        in_specs=placed,
        out_specs=P("tm", "row", None, None),
        check_vma=False,
    )
```

```python
import functools

import jax
import jax.numpy as jnp
from jax import lax
from jax.experimental import pallas as pl
from jax.experimental.pallas import tpu as pltpu
from jax.sharding import PartitionSpec as P

D = 768
HEADS = 12
NSTATE = 16
GW = 16
INNER = 768
CONV_CH = 800
F = 8
T = F * GW
GROUP = 16
SPAN = 128
WAVES = 4
CELLS = GW // WAVES
ROWS = CELLS * F
PIECES = (0, 48, 80, 112, 128)
KEY = 0
STEP = 32

NT = ((1,), (1,))
TN = ((0,), (0,))
f32 = jnp.float32
bf16 = jnp.bfloat16


def lanes(rows):
    return lax.broadcasted_iota(jnp.int32, (rows, 128), 1)


def dot(a, b, dims=((1,), (0,)), precision=None):
    return lax.dot_general(a, b, (dims, ((), ())), preferred_element_type=f32, precision=precision)


def cell_major():
    r = lax.broadcasted_iota(jnp.int32, (T, T), 0)
    s = lax.broadcasted_iota(jnp.int32, (T, T), 1)
    return jnp.where(s == (r & (F - 1)) * GW + (r >> 3), 1.0, 0.0).astype(bf16)


def frame_major():
    r = lax.broadcasted_iota(jnp.int32, (T, T), 0)
    s = lax.broadcasted_iota(jnp.int32, (T, T), 1)
    return jnp.where(s == (r & (GW - 1)) * F + (r >> 4), 1.0, 0.0).astype(bf16)


def silu(x):
    return x / (1.0 + jnp.exp(-x))


def softplus(x):
    return jnp.maximum(x, 0.0) + jnp.log1p(jnp.exp(-jnp.abs(x)))


def convolve(wave, rows, taps, bias):
    low, high = ROWS * wave, ROWS * (wave + 1)

    def part(j, start, stop):
        z = [r(start, stop) for r in rows]
        return taps[0][j] * z[0] + taps[1][j] * z[1] + taps[2][j] * z[2]

    edge = jnp.zeros((F, bias.shape[1]), f32)
    if wave == 0:
        left = jnp.concatenate([edge, part(0, low, high - F)], axis=0)
    else:
        left = part(0, low - F, high - F)
    if wave == WAVES - 1:
        right = jnp.concatenate([part(2, low + F, high), edge], axis=0)
    else:
        right = part(2, low + F, high + F)
    return silu(part(1, low, high) + left + right + bias)


def packets(tiles):
    return jnp.concatenate([t.reshape(-1, F, 128) for t in tiles], axis=1).astype(bf16)


def unpack(block, j):
    return block[:, F * j : F * (j + 1)].reshape(SPAN, 128)


def kernel(
    n_tm,
    n_row,
    tok_hbm,
    mix_hbm,
    gate_hbm,
    out_hbm,
    taps_hbm,
    cbias_hbm,
    gain_hbm,
    sbias_ref,
    rate_ref,
    skip_ref,
    o_ref,
    tok,
    halo,
    mixw,
    gatew,
    outw,
    taps_ref,
    cbias_ref,
    gain_ref,
    mine,
    center,
    side,
    value,
    gate,
    send_e,
    recv_e,
    send_a,
    recv_a,
    send_b,
    recv_b,
    state_out,
    state_in,
    fade_out,
    fade_in,
    send2,
    recv2,
    load_sem,
    halo_send,
    halo_recv,
    one_send,
    one_recv,
    state_send,
    state_recv,
    two_send,
    two_recv,
):
    me = lax.axis_index("tm")
    row = lax.axis_index("row")
    up = lax.rem(row + 1, n_row)
    down = lax.rem(row + n_row - 1, n_row)
    n_groups = n_tm // GROUP
    group = me // GROUP
    member = lax.rem(me, GROUP)
    chip = member // 2
    core = lax.rem(member, 2)
    my_wave = 2 * core + lax.rem(chip, 2)
    cell = CELLS * my_wave + chip // 2

    def peer(i):
        return lax.rem(member + i, GROUP)

    barrier = pltpu.get_barrier_semaphore()
    for other in (up, down):
        pl.semaphore_signal(barrier, inc=1, device_id={"row": other})

    for i in range(1, GROUP):
        far = GROUP // 2 + (i // 2 if i % 2 else -(i // 2))
        pl.semaphore_signal(barrier, inc=1, device_id={"tm": group * GROUP + peer(far)})
    for i in range(1, n_groups):
        pl.semaphore_signal(barrier, inc=1, device_id={"tm": lax.rem(me + GROUP * i, n_tm)})

    loads = [
        pltpu.make_async_copy(src, dst, load_sem.at[i])
        for i, (src, dst) in enumerate(
            (
                (tok_hbm, tok),
                (gate_hbm, gatew),
                (mix_hbm, mixw),
                (taps_hbm, taps_ref),
                (cbias_hbm, cbias_ref),
                (gain_hbm, gain_ref),
                (out_hbm, outw),
            )
        )
    ]
    for load in loads:
        load.start()
    perm = cell_major()
    loads[0].wait()
    own = dot(perm, tok[...]).astype(bf16)
    mine[...] = own
    pl.semaphore_wait(barrier, 2 + GROUP - 1 + n_groups - 1)

    pieces = [pl.ds(a, b - a) for a, b in zip(PIECES[:-1], PIECES[1:])]
    halos = [
        [
            pltpu.make_async_remote_copy(
                src_ref=mine.at[piece],
                dst_ref=halo.at[i, piece],
                send_sem=halo_send.at[i, w],
                recv_sem=halo_recv.at[i, w],
                device_id={"row": other},
            )
            for i, other in enumerate((up, down))
        ]
        for w, piece in enumerate(pieces)
    ]
    for pair in halos:
        for copy in pair:
            copy.start()

    loads[1].wait()
    gs = dot(own, gatew[...], NT).astype(bf16).astype(f32)
    gate[...] = gs[:, :INNER]
    steps = jnp.concatenate([gs[:, INNER:], jnp.zeros((T, 128 - HEADS), f32)], axis=1)
    steps = pltpu.roll(steps, STEP, 1)
    loads[2].wait()
    center[...] = dot(own, mixw[...], NT).astype(bf16).astype(f32)
    for load in loads[3:5]:
        load.wait()

    def activated(wave, sides, start, size):
        z = dot(sides, mixw[start : start + size, :], NT).astype(bf16).astype(f32)
        n = z.shape[0] // 2
        cols = slice(start, start + size)
        new = slice(PIECES[wave], PIECES[wave + 1])
        side[0, new, cols] = jnp.where(row > 0, z[:n], 0.0)
        side[1, new, cols] = jnp.where(row < n_row - 1, z[n:], 0.0)
        taps = [[taps_ref[i, j : j + 1, cols] for j in range(3)] for i in range(3)]
        rows = [
            lambda a, b: side[0, a:b, cols],
            lambda a, b: center[a:b, cols],
            lambda a, b: side[1, a:b, cols],
        ]
        return convolve(wave, rows, taps, cbias_ref[cols].reshape(1, size))

    def send_wave(wave, send, recv, which):
        def target(k):
            return 4 * k + 2 * (wave % 2) + wave // 2

        def copy(k):
            return pltpu.make_async_remote_copy(
                src_ref=send.at[CELLS * wave + k],
                dst_ref=recv.at[member],
                send_sem=one_send.at[which],
                recv_sem=one_recv.at[which],
                device_id={"tm": group * GROUP + target(k)},
            )

        own_k = chip // 2
        for i in range(1, CELLS):
            copy(lax.rem(own_k + i, CELLS)).start()

        @pl.when(my_wave == wave)
        def _():
            recv[member] = send[cell]

        @pl.when(my_wave != wave)
        def _():
            copy(own_k).start()

    def return_all(send, recv, send_sem, recv_sem):
        def one(i, c):
            other = peer(i)
            pltpu.make_async_remote_copy(
                src_ref=send.at[other],
                dst_ref=recv.at[cell],
                send_sem=send_sem,
                recv_sem=recv_sem,
                device_id={"tm": group * GROUP + other},
            ).start()
            return c

        lax.fori_loop(1, GROUP, one, 0)
        recv[cell] = send[member]

    def wait_all(buf, sem, count=GROUP - 1):
        every = buf.at[pl.ds(0, count)]
        pltpu.make_async_copy(every, every, sem).wait()

    for wave in range(WAVES):
        for copy in halos[wave]:
            copy.wait_recv()
        rows = slice(ROWS * wave, ROWS * (wave + 1))
        cells = slice(CELLS * wave, CELLS * (wave + 1))
        sides = halo[:, PIECES[wave] : PIECES[wave + 1]].reshape(-1, D)
        key = activated(wave, sides, INNER, 32)
        key = jnp.concatenate([key, jnp.zeros((ROWS, 96), f32)], axis=1)
        extra = jnp.where(lanes(ROWS) < STEP, key, steps[rows])
        late = pltpu.roll(extra, 64, 1).reshape(CELLS, F, 128)[:, F // 2 :]
        early = extra.reshape(CELLS, F, 128)[:, : F // 2]
        front = lax.broadcasted_iota(jnp.int32, early.shape, 2) < 64
        send_e[cells] = jnp.where(front, early, late)
        send_wave(wave, send_e, recv_e, 0)
        act = activated(wave, sides, 0, 512)
        value[rows, :512] = act
        send_a[cells] = packets([act[:, 128 * j : 128 * (j + 1)] for j in range(4)])
        send_wave(wave, send_a, recv_a, 1)
        act = activated(wave, sides, 512, 256)
        value[rows, 512:] = act
        send_b[cells] = packets([act[:, 128 * j : 128 * (j + 1)] for j in range(2)])
        send_wave(wave, send_b, recv_b, 2)

    lane = lanes(1)
    bias_lane = jnp.zeros((1, 128), f32)
    rate_lane = jnp.zeros((1, 128), f32)
    for h in range(HEADS):
        bias_lane = jnp.where(lane == STEP + h, sbias_ref[h], bias_lane)
        rate_lane = jnp.where(lane == STEP + h, rate_ref[h], rate_lane)
    r = lax.broadcasted_iota(jnp.int32, (SPAN, SPAN), 0)
    s = lax.broadcasted_iota(jnp.int32, (SPAN, SPAN), 1)
    past = s <= r
    half = lanes(SPAN) < 64

    def col(a, h):
        return a[:, STEP + h : STEP + h + 1]

    def both(a, j):
        return jnp.where(half[: a.shape[0]], col(a, 2 * j), col(a, 2 * j + 1))

    blocks = (pl.ds(0, 2), pl.ds(2, 1))

    def send_state(part):
        for i in range(1, n_groups):
            pltpu.make_async_remote_copy(
                src_ref=state_out.at[blocks[part]],
                dst_ref=state_in.at[i - 1, blocks[part]],
                send_sem=state_send.at[part],
                recv_sem=state_recv.at[part],
                device_id={"tm": lax.rem(me + GROUP * i, n_tm)},
            ).start()

    def wait_state(part, sem):
        every = state_in.at[pl.ds(0, n_groups - 1), blocks[part]]
        pltpu.make_async_copy(every, every, sem).wait()

    wait_all(recv_e, one_recv.at[0])
    early = recv_e[...]
    extra = jnp.concatenate([early, pltpu.roll(early, 64, 2)], axis=1).reshape(SPAN, 128)
    step = softplus(extra + bias_lane)
    tri = jnp.where(past, 1.0, 0.0).astype(f32)
    cum = dot(tri, -step * rate_lane, precision=lax.Precision.HIGHEST)
    end = cum[SPAN - 1 :, :]
    fade_out[...] = jnp.broadcast_to(end, (8, 128))
    for i in range(1, n_groups):
        pltpu.make_async_remote_copy(
            src_ref=fade_out,
            dst_ref=fade_in.at[i - 1],
            send_sem=state_send.at[2],
            recv_sem=state_recv.at[2],
            device_id={"tm": lax.rem(me + GROUP * i, n_tm)},
        ).start()
    weight = jnp.exp(end - cum) * step
    write = extra[:, :NSTATE].astype(bf16)
    read = extra[:, NSTATE : 2 * NSTATE].astype(bf16)

    def local_state(j, x):
        scaled = jnp.concatenate([x[k] * both(weight, j + k) for k in range(2)], axis=1)
        state_out[j // 2] = dot(write, scaled.astype(bf16), TN).astype(bf16)

    wait_all(recv_a, one_recv.at[1])
    block = recv_a[...].astype(f32)
    x = [unpack(block, j) for j in range(4)]
    local_state(0, x[:2])
    local_state(2, x[2:])
    send_state(0)
    wait_all(recv_b, one_recv.at[2])
    block = recv_b[...].astype(f32)
    x = x + [unpack(block, j) for j in range(2)]
    local_state(4, x[4:])
    send_state(1)

    late = jnp.transpose(jnp.log(step) - cum)
    reach = jnp.exp(cum)
    pair = dot(read, write, NT)
    inner = []
    for j in range(6):
        xb = x[j].astype(bf16)
        part = []
        for h in (2 * j, 2 * j + 1):
            span = col(cum, h) + late[STEP + h : STEP + h + 1, :]
            m = pair * jnp.exp(jnp.where(past, span, -1e30))
            part.append(dot(m.astype(bf16), xb))
        inner.append(jnp.where(half, part[0], part[1]))

    wait_all(fade_in, state_recv.at[2], n_groups - 1)
    fades = [jnp.exp(fade_in[i][:1]) for i in range(n_groups - 1)]

    def carried(block):
        total = jnp.zeros((NSTATE, 256), f32)
        for i in range(n_groups - 2, -1, -1):
            fade = jnp.concatenate([both(fades[i], 2 * block + k) for k in range(2)], axis=1)
            total = jnp.where(group > i, total * fade + state_in[i, block].astype(f32), 0.0)
        return dot(read, total.astype(bf16))

    def send_back(third, tiles):
        send2[third] = packets(tiles)
        return_all(send2.at[third], recv2.at[third], two_send.at[third], two_recv.at[third])

    def results(block):
        rest = carried(block)
        return [
            inner[2 * block + k] + both(reach, 2 * block + k) * rest[:, 128 * k : 128 * (k + 1)]
            for k in range(2)
        ]

    wait_state(0, state_recv.at[0])
    send_back(0, results(0))
    send_back(1, results(1))
    wait_state(1, state_recv.at[1])
    send_back(2, results(2))

    loads[5].wait()
    lane = lanes(1)
    gated = []
    total = jnp.zeros((T, 1), f32)
    for third in range(3):
        wait_all(recv2.at[third], two_recv.at[third])
        block = recv2[third].astype(f32)
        for k in range(2):
            j = 2 * third + k
            cut = slice(128 * j, 128 * (j + 1))
            skip = jnp.where(lane < 64, skip_ref[2 * j], skip_ref[2 * j + 1])
            g = (unpack(block, k) + skip * value[:, cut]) * silu(gate[:, cut])
            total = total + jnp.sum(g * g, axis=-1, keepdims=True)
            gated.append(g * gain_ref[cut].reshape(1, 128))
    scale = lax.rsqrt(total * (1.0 / INNER) + 1e-5)
    normed = jnp.concatenate([g * scale for g in gated], axis=1).astype(bf16)
    normed = dot(frame_major(), normed).astype(bf16)
    loads[6].wait()
    o_ref[...] = (tok[...].astype(f32) + dot(normed, outw[...])).astype(bf16)

    for pair in halos:
        for copy in pair:
            copy.wait_send()
    for i, buf in enumerate((send_e, send_a, send_b)):
        wait_all(buf, one_send.at[i])
    for part in range(2):
        wait_state(part, state_send.at[part])
    wait_all(fade_in, state_send.at[2], n_groups - 1)
    for third in range(3):
        wait_all(send2.at[third], two_send.at[third])


def per_device(
    n_tm,
    n_row,
    depth_tokens,
    mixer_weight,
    gate_weight,
    conv_kernel,
    conv_bias,
    step_bias,
    decay_rate,
    skip_gain,
    norm_gain,
    out_weight,
):
    hbm = pl.BlockSpec(memory_space=pltpu.HBM)
    vmem = pl.BlockSpec(memory_space=pltpu.VMEM)
    smem = pl.BlockSpec(memory_space=pltpu.SMEM)
    dma = pltpu.SemaphoreType.DMA
    n_groups = n_tm // GROUP
    out = pl.pallas_call(
        functools.partial(kernel, n_tm, n_row),
        out_shape=pltpu.VMEM((T, D), bf16),
        in_specs=[hbm] * 7 + [smem] * 3,
        out_specs=vmem,
        scratch_shapes=[
            pltpu.VMEM((T, D), bf16),
            pltpu.VMEM((2, T, D), bf16),
            pltpu.VMEM((CONV_CH, D), bf16),
            pltpu.VMEM((INNER + HEADS, D), bf16),
            pltpu.VMEM((INNER, D), bf16),
            pltpu.VMEM((3, 3, CONV_CH), f32),
            pltpu.VMEM((CONV_CH,), f32),
            pltpu.VMEM((INNER,), f32),
            pltpu.VMEM((T, D), bf16),
            pltpu.VMEM((T, CONV_CH), f32),
            pltpu.VMEM((2, T, CONV_CH), f32),
            pltpu.VMEM((T, INNER), f32),
            pltpu.VMEM((T, INNER), f32),
            pltpu.VMEM((GROUP, F // 2, 128), f32),
            pltpu.VMEM((GROUP, F // 2, 128), f32),
            pltpu.VMEM((GROUP, 4 * F, 128), bf16),
            pltpu.VMEM((GROUP, 4 * F, 128), bf16),
            pltpu.VMEM((GROUP, 2 * F, 128), bf16),
            pltpu.VMEM((GROUP, 2 * F, 128), bf16),
            pltpu.VMEM((3, NSTATE, 256), bf16),
            pltpu.VMEM((n_groups - 1, 3, NSTATE, 256), bf16),
            pltpu.VMEM((8, 128), f32),
            pltpu.VMEM((n_groups - 1, 8, 128), f32),
            pltpu.VMEM((3, GROUP, 2 * F, 128), bf16),
            pltpu.VMEM((3, GROUP, 2 * F, 128), bf16),
            dma((7,)),
            dma((2, WAVES)),
            dma((2, WAVES)),
            dma((3,)),
            dma((3,)),
            dma((3,)),
            dma((3,)),
            dma((3,)),
            dma((3,)),
        ],
        compiler_params=pltpu.CompilerParams(
            collective_id=0, has_side_effects=True, vmem_limit_bytes=56 * 1024 * 1024
        ),
    )(
        depth_tokens.reshape(T, D),
        mixer_weight.T,
        gate_weight.T,
        out_weight,
        conv_kernel,
        conv_bias,
        norm_gain,
        step_bias,
        decay_rate,
        skip_gain,
    )
    return out.reshape(depth_tokens.shape)


def solution(mesh):
    placed = (P("tm", "row", None, None), P(), P(), P(), P(), P(), P(), P(), P(), P())
    return jax.shard_map(
        functools.partial(per_device, mesh.shape["tm"], mesh.shape["row"]),
        mesh=mesh,
        in_specs=placed,
        out_specs=P("tm", "row", None, None),
        check_vma=False,
    )
```

```python
import functools

import jax
import jax.numpy as jnp
from jax import lax
from jax.experimental import pallas as pl
from jax.experimental.pallas import tpu as pltpu
from jax.sharding import PartitionSpec as P

D = 768
HEADS = 12
NSTATE = 16
GW = 16
INNER = 768
CONV_CH = 800
F = 8
T = F * GW
GROUP = 16
SPAN = 128
WAVES = 4
CELLS = GW // WAVES
ROWS = CELLS * F
PIECES = (0, 48, 80, 112, 128)
KEY = 0
STEP = 32

NT = ((1,), (1,))
TN = ((0,), (0,))
f32 = jnp.float32
bf16 = jnp.bfloat16


def lanes(rows):
    return lax.broadcasted_iota(jnp.int32, (rows, 128), 1)


def dot(a, b, dims=((1,), (0,)), precision=None):
    return lax.dot_general(a, b, (dims, ((), ())), preferred_element_type=f32, precision=precision)


def cell_major():
    r = lax.broadcasted_iota(jnp.int32, (T, T), 0)
    s = lax.broadcasted_iota(jnp.int32, (T, T), 1)
    return jnp.where(s == (r & (F - 1)) * GW + (r >> 3), 1.0, 0.0).astype(bf16)


def frame_major():
    r = lax.broadcasted_iota(jnp.int32, (T, T), 0)
    s = lax.broadcasted_iota(jnp.int32, (T, T), 1)
    return jnp.where(s == (r & (GW - 1)) * F + (r >> 4), 1.0, 0.0).astype(bf16)


def silu(x):
    return x / (1.0 + jnp.exp(-x))


def softplus(x):
    return jnp.maximum(x, 0.0) + jnp.log1p(jnp.exp(-jnp.abs(x)))


def convolve(wave, rows, taps, bias):
    low, high = ROWS * wave, ROWS * (wave + 1)

    def part(j, start, stop):
        z = [r(start, stop) for r in rows]
        return taps[0][j] * z[0] + taps[1][j] * z[1] + taps[2][j] * z[2]

    edge = jnp.zeros((F, bias.shape[1]), f32)
    if wave == 0:
        left = jnp.concatenate([edge, part(0, low, high - F)], axis=0)
    else:
        left = part(0, low - F, high - F)
    if wave == WAVES - 1:
        right = jnp.concatenate([part(2, low + F, high), edge], axis=0)
    else:
        right = part(2, low + F, high + F)
    return silu(part(1, low, high) + left + right + bias)


def packets(tiles):
    return jnp.concatenate([t.reshape(-1, F, 128) for t in tiles], axis=1).astype(bf16)


def unpack(block, j):
    return block[:, F * j : F * (j + 1)].reshape(SPAN, 128)


def kernel(
    n_tm,
    n_row,
    tok_hbm,
    mix_hbm,
    gate_hbm,
    out_hbm,
    taps_hbm,
    cbias_hbm,
    gain_hbm,
    sbias_ref,
    rate_ref,
    skip_ref,
    o_ref,
    tok,
    halo,
    mixw,
    gatew,
    outw,
    taps_ref,
    cbias_ref,
    gain_ref,
    mine,
    center,
    side,
    value,
    gate,
    send_e,
    recv_e,
    send_a,
    recv_a,
    send_b,
    recv_b,
    state_out,
    state_in,
    fade_out,
    fade_in,
    send2,
    recv2,
    ready,
    load_sem,
    halo_send,
    halo_recv,
    one_send,
    one_recv,
    state_send,
    state_recv,
    two_send,
    two_recv,
):
    me = lax.axis_index("tm")
    row = lax.axis_index("row")
    n_groups = n_tm // GROUP
    group = me // GROUP
    member = lax.rem(me, GROUP)
    chip = member // 2
    core = lax.rem(member, 2)
    my_wave = 2 * core + lax.rem(chip, 2)
    cell = CELLS * my_wave + chip // 2

    def peer(i):
        return lax.rem(member + i, GROUP)

    later = [(i, group + i < n_groups, me + GROUP * i) for i in range(1, n_groups)]
    earlier = [(i, group >= i, me - GROUP * i) for i in range(1, n_groups)]
    has_down, has_up = row > 0, row < n_row - 1
    toward = ((has_up, row + 1), (has_down, row - 1))
    origin = (has_down, has_up)

    barrier = pltpu.get_barrier_semaphore()
    for exists, other in toward:

        @pl.when(exists)
        def _():
            pl.semaphore_signal(barrier, inc=1, device_id={"row": other})

    for i in range(1, GROUP):
        far = GROUP // 2 + (i // 2 if i % 2 else -(i // 2))
        pl.semaphore_signal(barrier, inc=1, device_id={"tm": group * GROUP + peer(far)})
    for i, exists, other in later:

        @pl.when(exists)
        def _():
            pl.semaphore_signal(barrier, inc=1, device_id={"tm": other})

    loads = [
        pltpu.make_async_copy(src, dst, load_sem.at[i])
        for i, (src, dst) in enumerate(
            (
                (tok_hbm, tok),
                (gate_hbm, gatew),
                (mix_hbm, mixw),
                (taps_hbm, taps_ref),
                (cbias_hbm, cbias_ref),
                (gain_hbm, gain_ref),
                (out_hbm, outw),
            )
        )
    ]
    for load in loads:
        load.start()
    perm = cell_major()
    loads[0].wait()
    own = dot(perm, tok[...]).astype(bf16)
    mine[...] = own
    neighbours = jnp.minimum(row, 1) + jnp.minimum(n_row - 1 - row, 1)
    pl.semaphore_wait(barrier, GROUP - 1 + group + neighbours)
    for i, exists, other in earlier:

        @pl.when(exists)
        def _():
            pl.semaphore_signal(ready.at[i - 1], inc=1, device_id={"tm": other})


    pieces = [pl.ds(a, b - a) for a, b in zip(PIECES[:-1], PIECES[1:])]
    halos = [
        [
            pltpu.make_async_remote_copy(
                src_ref=mine.at[piece],
                dst_ref=halo.at[i, piece],
                send_sem=halo_send.at[i, w],
                recv_sem=halo_recv.at[i, w],
                device_id={"row": other},
            )
            for i, (_, other) in enumerate(toward)
        ]
        for w, piece in enumerate(pieces)
    ]
    for pair in halos:
        for (exists, _), copy in zip(toward, pair):
            pl.when(exists)(copy.start)

    loads[1].wait()
    gs = dot(own, gatew[...], NT).astype(bf16).astype(f32)
    gate[...] = gs[:, :INNER]
    steps = jnp.concatenate([gs[:, INNER:], jnp.zeros((T, 128 - HEADS), f32)], axis=1)
    steps = pltpu.roll(steps, STEP, 1)
    loads[2].wait()
    center[...] = dot(own, mixw[...], NT).astype(bf16).astype(f32)
    for load in loads[3:5]:
        load.wait()

    def activated(wave, sides, start, size):
        z = dot(sides, mixw[start : start + size, :], NT).astype(bf16).astype(f32)
        n = z.shape[0] // 2
        cols = slice(start, start + size)
        new = slice(PIECES[wave], PIECES[wave + 1])
        side[0, new, cols] = jnp.where(has_down, z[:n], 0.0)
        side[1, new, cols] = jnp.where(has_up, z[n:], 0.0)
        taps = [[taps_ref[i, j : j + 1, cols] for j in range(3)] for i in range(3)]
        rows = [
            lambda a, b: side[0, a:b, cols],
            lambda a, b: center[a:b, cols],
            lambda a, b: side[1, a:b, cols],
        ]
        return convolve(wave, rows, taps, cbias_ref[cols].reshape(1, size))

    def send_wave(wave, send, recv, which):
        def target(k):
            return 4 * k + 2 * (wave % 2) + wave // 2

        def copy(k):
            return pltpu.make_async_remote_copy(
                src_ref=send.at[CELLS * wave + k],
                dst_ref=recv.at[member],
                send_sem=one_send.at[which],
                recv_sem=one_recv.at[which],
                device_id={"tm": group * GROUP + target(k)},
            )

        own_k = chip // 2
        for i in range(1, CELLS):
            copy(lax.rem(own_k + i, CELLS)).start()

        @pl.when(my_wave == wave)
        def _():
            recv[member] = send[cell]

        @pl.when(my_wave != wave)
        def _():
            copy(own_k).start()

    def return_all(send, recv, send_sem, recv_sem):
        def one(i, c):
            other = peer(i)
            pltpu.make_async_remote_copy(
                src_ref=send.at[other],
                dst_ref=recv.at[cell],
                send_sem=send_sem,
                recv_sem=recv_sem,
                device_id={"tm": group * GROUP + other},
            ).start()
            return c

        lax.fori_loop(1, GROUP, one, 0)
        recv[cell] = send[member]

    def wait_all(buf, sem, count=GROUP - 1):
        every = buf.at[pl.ds(0, count)]
        pltpu.make_async_copy(every, every, sem).wait()

    for wave in range(WAVES):
        for exists, copy in zip(origin, halos[wave]):
            pl.when(exists)(copy.wait_recv)
        rows = slice(ROWS * wave, ROWS * (wave + 1))
        cells = slice(CELLS * wave, CELLS * (wave + 1))
        sides = halo[:, PIECES[wave] : PIECES[wave + 1]].reshape(-1, D)
        key = activated(wave, sides, INNER, 32)
        key = jnp.concatenate([key, jnp.zeros((ROWS, 96), f32)], axis=1)
        extra = jnp.where(lanes(ROWS) < STEP, key, steps[rows])
        late = pltpu.roll(extra, 64, 1).reshape(CELLS, F, 128)[:, F // 2 :]
        early = extra.reshape(CELLS, F, 128)[:, : F // 2]
        front = lax.broadcasted_iota(jnp.int32, early.shape, 2) < 64
        send_e[cells] = jnp.where(front, early, late)
        send_wave(wave, send_e, recv_e, 0)
        act = activated(wave, sides, 0, 512)
        value[rows, :512] = act
        send_a[cells] = packets([act[:, 128 * j : 128 * (j + 1)] for j in range(4)])
        send_wave(wave, send_a, recv_a, 1)
        act = activated(wave, sides, 512, 256)
        value[rows, 512:] = act
        send_b[cells] = packets([act[:, 128 * j : 128 * (j + 1)] for j in range(2)])
        send_wave(wave, send_b, recv_b, 2)

    lane = lanes(1)
    bias_lane = jnp.zeros((1, 128), f32)
    rate_lane = jnp.zeros((1, 128), f32)
    for h in range(HEADS):
        bias_lane = jnp.where(lane == STEP + h, sbias_ref[h], bias_lane)
        rate_lane = jnp.where(lane == STEP + h, rate_ref[h], rate_lane)
    r = lax.broadcasted_iota(jnp.int32, (SPAN, SPAN), 0)
    s = lax.broadcasted_iota(jnp.int32, (SPAN, SPAN), 1)
    past = s <= r
    half = lanes(SPAN) < 64

    def col(a, h):
        return a[:, STEP + h : STEP + h + 1]

    def both(a, j):
        return jnp.where(half[: a.shape[0]], col(a, 2 * j), col(a, 2 * j + 1))

    blocks = (pl.ds(0, 2), pl.ds(2, 1))

    def state_copy(part, i, other):
        if part == 2:
            src, dst = fade_out, fade_in.at[i - 1]
        else:
            src, dst = state_out.at[blocks[part]], state_in.at[i - 1, blocks[part]]
        return pltpu.make_async_remote_copy(
            src_ref=src,
            dst_ref=dst,
            send_sem=state_send.at[part, i - 1],
            recv_sem=state_recv.at[part, i - 1],
            device_id={"tm": other},
        )

    def send_state(part):
        for i, exists, other in later:
            pl.when(exists)(state_copy(part, i, other).start)

    def wait_state(part):
        for i, exists, other in earlier:
            pl.when(exists)(state_copy(part, i, other).wait_recv)

    wait_all(recv_e, one_recv.at[0])
    early = recv_e[...]
    extra = jnp.concatenate([early, pltpu.roll(early, 64, 2)], axis=1).reshape(SPAN, 128)
    step = softplus(extra + bias_lane)
    tri = jnp.where(past, 1.0, 0.0).astype(f32)
    cum = dot(tri, -step * rate_lane, precision=lax.Precision.HIGHEST)
    end = cum[SPAN - 1 :, :]
    fade_out[...] = jnp.broadcast_to(end, (8, 128))
    for i, exists, other in later:

        @pl.when(exists)
        def _():
            pl.semaphore_wait(ready.at[i - 1], 1)

    send_state(2)
    weight = jnp.exp(end - cum) * step
    write = extra[:, :NSTATE].astype(bf16)
    read = extra[:, NSTATE : 2 * NSTATE].astype(bf16)

    def local_state(j, x):
        scaled = jnp.concatenate([x[k] * both(weight, j + k) for k in range(2)], axis=1)
        state_out[j // 2] = dot(write, scaled.astype(bf16), TN).astype(bf16)

    wait_all(recv_a, one_recv.at[1])
    block = recv_a[...].astype(f32)
    x = [unpack(block, j) for j in range(4)]
    local_state(0, x[:2])
    local_state(2, x[2:])
    send_state(0)
    wait_all(recv_b, one_recv.at[2])
    block = recv_b[...].astype(f32)
    x = x + [unpack(block, j) for j in range(2)]
    local_state(4, x[4:])
    send_state(1)

    late = jnp.transpose(jnp.log(step) - cum)
    reach = jnp.exp(cum)
    pair = dot(read, write, NT)
    inner = []
    for j in range(6):
        xb = x[j].astype(bf16)
        part = []
        for h in (2 * j, 2 * j + 1):
            span = col(cum, h) + late[STEP + h : STEP + h + 1, :]
            m = pair * jnp.exp(jnp.where(past, span, -1e30))
            part.append(dot(m.astype(bf16), xb))
        inner.append(jnp.where(half, part[0], part[1]))

    wait_state(2)
    fades = [jnp.exp(fade_in[i][:1]) for i in range(n_groups - 1)]

    def carried(block):
        total = jnp.zeros((NSTATE, 256), f32)
        for i in range(n_groups - 2, -1, -1):
            fade = jnp.concatenate([both(fades[i], 2 * block + k) for k in range(2)], axis=1)
            total = jnp.where(group > i, total * fade + state_in[i, block].astype(f32), 0.0)
        return dot(read, total.astype(bf16))

    def send_back(third, tiles):
        send2[third] = packets(tiles)
        return_all(send2.at[third], recv2.at[third], two_send.at[third], two_recv.at[third])

    def results(block):
        rest = carried(block)
        return [
            inner[2 * block + k] + both(reach, 2 * block + k) * rest[:, 128 * k : 128 * (k + 1)]
            for k in range(2)
        ]

    wait_state(0)
    send_back(0, results(0))
    send_back(1, results(1))
    wait_state(1)
    send_back(2, results(2))

    loads[5].wait()
    lane = lanes(1)
    gated = []
    total = jnp.zeros((T, 1), f32)
    for third in range(3):
        wait_all(recv2.at[third], two_recv.at[third])
        block = recv2[third].astype(f32)
        for k in range(2):
            j = 2 * third + k
            cut = slice(128 * j, 128 * (j + 1))
            skip = jnp.where(lane < 64, skip_ref[2 * j], skip_ref[2 * j + 1])
            g = (unpack(block, k) + skip * value[:, cut]) * silu(gate[:, cut])
            total = total + jnp.sum(g * g, axis=-1, keepdims=True)
            gated.append(g * gain_ref[cut].reshape(1, 128))
    scale = lax.rsqrt(total * (1.0 / INNER) + 1e-5)
    normed = jnp.concatenate([g * scale for g in gated], axis=1).astype(bf16)
    normed = dot(frame_major(), normed).astype(bf16)
    loads[6].wait()
    o_ref[...] = (tok[...].astype(f32) + dot(normed, outw[...])).astype(bf16)

    for pair in halos:
        for (exists, _), copy in zip(toward, pair):
            pl.when(exists)(copy.wait_send)
    for i, buf in enumerate((send_e, send_a, send_b)):
        wait_all(buf, one_send.at[i])
    for part in range(3):
        for i, exists, other in later:
            pl.when(exists)(state_copy(part, i, other).wait_send)
    for third in range(3):
        wait_all(send2.at[third], two_send.at[third])


def per_device(
    n_tm,
    n_row,
    depth_tokens,
    mixer_weight,
    gate_weight,
    conv_kernel,
    conv_bias,
    step_bias,
    decay_rate,
    skip_gain,
    norm_gain,
    out_weight,
):
    hbm = pl.BlockSpec(memory_space=pltpu.HBM)
    vmem = pl.BlockSpec(memory_space=pltpu.VMEM)
    smem = pl.BlockSpec(memory_space=pltpu.SMEM)
    dma = pltpu.SemaphoreType.DMA
    n_groups = n_tm // GROUP
    out = pl.pallas_call(
        functools.partial(kernel, n_tm, n_row),
        out_shape=pltpu.VMEM((T, D), bf16),
        in_specs=[hbm] * 7 + [smem] * 3,
        out_specs=vmem,
        scratch_shapes=[
            pltpu.VMEM((T, D), bf16),
            pltpu.VMEM((2, T, D), bf16),
            pltpu.VMEM((CONV_CH, D), bf16),
            pltpu.VMEM((INNER + HEADS, D), bf16),
            pltpu.VMEM((INNER, D), bf16),
            pltpu.VMEM((3, 3, CONV_CH), f32),
            pltpu.VMEM((CONV_CH,), f32),
            pltpu.VMEM((INNER,), f32),
            pltpu.VMEM((T, D), bf16),
            pltpu.VMEM((T, CONV_CH), f32),
            pltpu.VMEM((2, T, CONV_CH), f32),
            pltpu.VMEM((T, INNER), f32),
            pltpu.VMEM((T, INNER), f32),
            pltpu.VMEM((GROUP, F // 2, 128), f32),
            pltpu.VMEM((GROUP, F // 2, 128), f32),
            pltpu.VMEM((GROUP, 4 * F, 128), bf16),
            pltpu.VMEM((GROUP, 4 * F, 128), bf16),
            pltpu.VMEM((GROUP, 2 * F, 128), bf16),
            pltpu.VMEM((GROUP, 2 * F, 128), bf16),
            pltpu.VMEM((3, NSTATE, 256), bf16),
            pltpu.VMEM((n_groups - 1, 3, NSTATE, 256), bf16),
            pltpu.VMEM((8, 128), f32),
            pltpu.VMEM((n_groups - 1, 8, 128), f32),
            pltpu.VMEM((3, GROUP, 2 * F, 128), bf16),
            pltpu.VMEM((3, GROUP, 2 * F, 128), bf16),
            pltpu.SemaphoreType.REGULAR((n_groups - 1,)),
            dma((7,)),
            dma((2, WAVES)),
            dma((2, WAVES)),
            dma((3,)),
            dma((3,)),
            dma((3, n_groups - 1)),
            dma((3, n_groups - 1)),
            dma((3,)),
            dma((3,)),
        ],
        compiler_params=pltpu.CompilerParams(
            collective_id=0, has_side_effects=True, vmem_limit_bytes=56 * 1024 * 1024
        ),
    )(
        depth_tokens.reshape(T, D),
        mixer_weight.T,
        gate_weight.T,
        out_weight,
        conv_kernel,
        conv_bias,
        norm_gain,
        step_bias,
        decay_rate,
        skip_gain,
    )
    return out.reshape(depth_tokens.shape)


def solution(mesh):
    placed = (P("tm", "row", None, None), P(), P(), P(), P(), P(), P(), P(), P(), P())
    return jax.shard_map(
        functools.partial(per_device, mesh.shape["tm"], mesh.shape["row"]),
        mesh=mesh,
        in_specs=placed,
        out_specs=P("tm", "row", None, None),
        check_vma=False,
    )
```

```python
import functools

import jax
import jax.numpy as jnp
from jax import lax
from jax.experimental import pallas as pl
from jax.experimental.pallas import tpu as pltpu
from jax.sharding import PartitionSpec as P

D = 768
HEADS = 12
NSTATE = 16
GW = 16
INNER = 768
CONV_CH = 800
F = 8
T = F * GW
GROUP = 16
SPAN = 128
WAVES = 4
CELLS = GW // WAVES
ROWS = CELLS * F
PIECES = (0, 48, 80, 112, 128)
KEY = 0
STEP = 32

NT = ((1,), (1,))
TN = ((0,), (0,))
f32 = jnp.float32
bf16 = jnp.bfloat16


def lanes(rows):
    return lax.broadcasted_iota(jnp.int32, (rows, 128), 1)


def dot(a, b, dims=((1,), (0,)), precision=None):
    return lax.dot_general(a, b, (dims, ((), ())), preferred_element_type=f32, precision=precision)


def cell_major():
    r = lax.broadcasted_iota(jnp.int32, (T, T), 0)
    s = lax.broadcasted_iota(jnp.int32, (T, T), 1)
    return jnp.where(s == (r & (F - 1)) * GW + (r >> 3), 1.0, 0.0).astype(bf16)


def frame_major():
    r = lax.broadcasted_iota(jnp.int32, (T, T), 0)
    s = lax.broadcasted_iota(jnp.int32, (T, T), 1)
    return jnp.where(s == (r & (GW - 1)) * F + (r >> 4), 1.0, 0.0).astype(bf16)


def silu(x):
    return x / (1.0 + jnp.exp(-x))


def softplus(x):
    return jnp.maximum(x, 0.0) + jnp.log1p(jnp.exp(-jnp.abs(x)))


def convolve(wave, rows, taps, bias):
    low, high = ROWS * wave, ROWS * (wave + 1)

    def part(j, start, stop):
        z = [r(start, stop) for r in rows]
        return taps[0][j] * z[0] + taps[1][j] * z[1] + taps[2][j] * z[2]

    edge = jnp.zeros((F, bias.shape[1]), f32)
    if wave == 0:
        left = jnp.concatenate([edge, part(0, low, high - F)], axis=0)
    else:
        left = part(0, low - F, high - F)
    if wave == WAVES - 1:
        right = jnp.concatenate([part(2, low + F, high), edge], axis=0)
    else:
        right = part(2, low + F, high + F)
    return silu(part(1, low, high) + left + right + bias)


def packets(tiles):
    return jnp.concatenate([t.reshape(-1, F, 128) for t in tiles], axis=1).astype(bf16)


def unpack(block, j):
    return block[:, F * j : F * (j + 1)].reshape(SPAN, 128)


def kernel(
    n_tm,
    n_row,
    tok_hbm,
    mix_hbm,
    gate_hbm,
    out_hbm,
    taps_hbm,
    cbias_hbm,
    gain_hbm,
    sbias_ref,
    rate_ref,
    skip_ref,
    o_ref,
    tok,
    halo,
    mixw,
    gatew,
    outw,
    taps_ref,
    cbias_ref,
    gain_ref,
    mine,
    center,
    side,
    value,
    gate,
    send_e,
    recv_e,
    send_a,
    recv_a,
    send_b,
    recv_b,
    state_out,
    state_in,
    fade_out,
    fade_in,
    send2,
    recv2,
    ready,
    load_sem,
    halo_send,
    halo_recv,
    one_send,
    one_recv,
    state_send,
    state_recv,
    two_send,
    two_recv,
):
    me = lax.axis_index("tm")
    row = lax.axis_index("row")
    n_groups = n_tm // GROUP
    group = me // GROUP
    member = lax.rem(me, GROUP)
    chip = member // 2
    core = lax.rem(member, 2)
    my_wave = 2 * core + lax.rem(chip, 2)
    cell = CELLS * my_wave + chip // 2

    def peer(i):
        return lax.rem(member + i, GROUP)

    later = [(i, group + i < n_groups, me + GROUP * i) for i in range(1, n_groups)]
    earlier = [(i, group >= i, me - GROUP * i) for i in range(1, n_groups)]
    has_down, has_up = row > 0, row < n_row - 1
    toward = ((has_up, row + 1), (has_down, row - 1))
    origin = (has_down, has_up)

    loads = [
        pltpu.make_async_copy(src, dst, load_sem.at[i])
        for i, (src, dst) in enumerate(
            (
                (tok_hbm, tok),
                (gate_hbm, gatew),
                (mix_hbm, mixw),
                (taps_hbm, taps_ref),
                (cbias_hbm, cbias_ref),
                (gain_hbm, gain_ref),
                (out_hbm, outw),
            )
        )
    ]
    loads[0].start()

    barrier = pltpu.get_barrier_semaphore()
    for exists, other in toward:

        @pl.when(exists)
        def _():
            pl.semaphore_signal(barrier, inc=1, device_id={"row": other})

    def greet(i, c):
        pl.semaphore_signal(barrier, inc=1, device_id={"tm": group * GROUP + i})
        return c

    lax.fori_loop(member + 1, GROUP, greet, 0)
    for i, exists, other in later:

        @pl.when(exists)
        def _():
            pl.semaphore_signal(barrier, inc=1, device_id={"tm": other})

    for load in loads[1:]:
        load.start()
    perm = cell_major()
    loads[0].wait()
    own = dot(perm, tok[...]).astype(bf16)
    mine[...] = own
    neighbours = jnp.minimum(row, 1) + jnp.minimum(n_row - 1 - row, 1)
    pl.semaphore_wait(barrier, member + group + neighbours)

    pieces = [pl.ds(a, b - a) for a, b in zip(PIECES[:-1], PIECES[1:])]
    halos = [
        [
            pltpu.make_async_remote_copy(
                src_ref=mine.at[piece],
                dst_ref=halo.at[i, piece],
                send_sem=halo_send.at[i, w],
                recv_sem=halo_recv.at[i, w],
                device_id={"row": other},
            )
            for i, (_, other) in enumerate(toward)
        ]
        for w, piece in enumerate(pieces)
    ]
    for pair in halos:
        for (exists, _), copy in zip(toward, pair):
            pl.when(exists)(copy.start)

    def answer(i, c):
        pl.semaphore_signal(ready.at[0], inc=1, device_id={"tm": group * GROUP + i})
        return c

    lax.fori_loop(0, member, answer, 0)
    for i, exists, other in earlier:

        @pl.when(exists)
        def _():
            pl.semaphore_signal(ready.at[i], inc=1, device_id={"tm": other})

    loads[1].wait()
    gs = dot(own, gatew[...], NT).astype(bf16).astype(f32)
    gate[...] = gs[:, :INNER]
    steps = jnp.concatenate([gs[:, INNER:], jnp.zeros((T, 128 - HEADS), f32)], axis=1)
    steps = pltpu.roll(steps, STEP, 1)
    loads[2].wait()
    center[...] = dot(own, mixw[...], NT).astype(bf16).astype(f32)
    for load in loads[3:5]:
        load.wait()

    def activated(wave, sides, start, size):
        z = dot(sides, mixw[start : start + size, :], NT).astype(bf16).astype(f32)
        n = z.shape[0] // 2
        cols = slice(start, start + size)
        new = slice(PIECES[wave], PIECES[wave + 1])
        side[0, new, cols] = jnp.where(has_down, z[:n], 0.0)
        side[1, new, cols] = jnp.where(has_up, z[n:], 0.0)
        taps = [[taps_ref[i, j : j + 1, cols] for j in range(3)] for i in range(3)]
        rows = [
            lambda a, b: side[0, a:b, cols],
            lambda a, b: center[a:b, cols],
            lambda a, b: side[1, a:b, cols],
        ]
        return convolve(wave, rows, taps, cbias_ref[cols].reshape(1, size))

    def send_wave(wave, send, recv, which):
        def target(k):
            return 4 * k + 2 * (wave % 2) + wave // 2

        def copy(k):
            return pltpu.make_async_remote_copy(
                src_ref=send.at[CELLS * wave + k],
                dst_ref=recv.at[member],
                send_sem=one_send.at[which],
                recv_sem=one_recv.at[which],
                device_id={"tm": group * GROUP + target(k)},
            )

        own_k = chip // 2
        for i in range(1, CELLS):
            copy(lax.rem(own_k + i, CELLS)).start()

        @pl.when(my_wave == wave)
        def _():
            recv[member] = send[cell]

        @pl.when(my_wave != wave)
        def _():
            copy(own_k).start()

    def return_all(send, recv, send_sem, recv_sem):
        def one(i, c):
            other = peer(i)
            pltpu.make_async_remote_copy(
                src_ref=send.at[other],
                dst_ref=recv.at[cell],
                send_sem=send_sem,
                recv_sem=recv_sem,
                device_id={"tm": group * GROUP + other},
            ).start()
            return c

        lax.fori_loop(1, GROUP, one, 0)
        recv[cell] = send[member]

    def wait_all(buf, sem, count=GROUP - 1):
        every = buf.at[pl.ds(0, count)]
        pltpu.make_async_copy(every, every, sem).wait()

    @pl.when(member < GROUP - 1)
    def _():
        pl.semaphore_wait(ready.at[0], GROUP - 1 - member)

    for wave in range(WAVES):
        for exists, copy in zip(origin, halos[wave]):
            pl.when(exists)(copy.wait_recv)
        rows = slice(ROWS * wave, ROWS * (wave + 1))
        cells = slice(CELLS * wave, CELLS * (wave + 1))
        sides = halo[:, PIECES[wave] : PIECES[wave + 1]].reshape(-1, D)
        key = activated(wave, sides, INNER, 32)
        key = jnp.concatenate([key, jnp.zeros((ROWS, 96), f32)], axis=1)
        extra = jnp.where(lanes(ROWS) < STEP, key, steps[rows])
        late = pltpu.roll(extra, 64, 1).reshape(CELLS, F, 128)[:, F // 2 :]
        early = extra.reshape(CELLS, F, 128)[:, : F // 2]
        front = lax.broadcasted_iota(jnp.int32, early.shape, 2) < 64
        send_e[cells] = jnp.where(front, early, late)
        send_wave(wave, send_e, recv_e, 0)
        act = activated(wave, sides, 0, 512)
        value[rows, :512] = act
        send_a[cells] = packets([act[:, 128 * j : 128 * (j + 1)] for j in range(4)])
        send_wave(wave, send_a, recv_a, 1)
        act = activated(wave, sides, 512, 256)
        value[rows, 512:] = act
        send_b[cells] = packets([act[:, 128 * j : 128 * (j + 1)] for j in range(2)])
        send_wave(wave, send_b, recv_b, 2)

    lane = lanes(1)
    bias_lane = jnp.zeros((1, 128), f32)
    rate_lane = jnp.zeros((1, 128), f32)
    for h in range(HEADS):
        bias_lane = jnp.where(lane == STEP + h, sbias_ref[h], bias_lane)
        rate_lane = jnp.where(lane == STEP + h, rate_ref[h], rate_lane)
    r = lax.broadcasted_iota(jnp.int32, (SPAN, SPAN), 0)
    s = lax.broadcasted_iota(jnp.int32, (SPAN, SPAN), 1)
    past = s <= r
    half = lanes(SPAN) < 64

    def col(a, h):
        return a[:, STEP + h : STEP + h + 1]

    def both(a, j):
        return jnp.where(half[: a.shape[0]], col(a, 2 * j), col(a, 2 * j + 1))

    blocks = (pl.ds(0, 2), pl.ds(2, 1))

    def state_copy(part, i, other):
        if part == 2:
            src, dst = fade_out, fade_in.at[i - 1]
        else:
            src, dst = state_out.at[blocks[part]], state_in.at[i - 1, blocks[part]]
        return pltpu.make_async_remote_copy(
            src_ref=src,
            dst_ref=dst,
            send_sem=state_send.at[part, i - 1],
            recv_sem=state_recv.at[part, i - 1],
            device_id={"tm": other},
        )

    def send_state(part):
        for i, exists, other in later:
            pl.when(exists)(state_copy(part, i, other).start)

    def wait_state(part):
        for i, exists, other in earlier:
            pl.when(exists)(state_copy(part, i, other).wait_recv)

    wait_all(recv_e, one_recv.at[0])
    early = recv_e[...]
    extra = jnp.concatenate([early, pltpu.roll(early, 64, 2)], axis=1).reshape(SPAN, 128)
    step = softplus(extra + bias_lane)
    tri = jnp.where(past, 1.0, 0.0).astype(f32)
    cum = dot(tri, -step * rate_lane, precision=lax.Precision.HIGHEST)
    end = cum[SPAN - 1 :, :]
    fade_out[...] = jnp.broadcast_to(end, (8, 128))
    for i, exists, other in later:

        @pl.when(exists)
        def _():
            pl.semaphore_wait(ready.at[i], 1)

    send_state(2)
    weight = jnp.exp(end - cum) * step
    write = extra[:, :NSTATE].astype(bf16)
    read = extra[:, NSTATE : 2 * NSTATE].astype(bf16)

    def local_state(j, x):
        scaled = jnp.concatenate([x[k] * both(weight, j + k) for k in range(2)], axis=1)
        state_out[j // 2] = dot(write, scaled.astype(bf16), TN).astype(bf16)

    wait_all(recv_a, one_recv.at[1])
    block = recv_a[...].astype(f32)
    x = [unpack(block, j) for j in range(4)]
    local_state(0, x[:2])
    local_state(2, x[2:])
    send_state(0)
    wait_all(recv_b, one_recv.at[2])
    block = recv_b[...].astype(f32)
    x = x + [unpack(block, j) for j in range(2)]
    local_state(4, x[4:])
    send_state(1)

    late = jnp.transpose(jnp.log(step) - cum)
    reach = jnp.exp(cum)
    pair = dot(read, write, NT)
    inner = []
    for j in range(6):
        xb = x[j].astype(bf16)
        part = []
        for h in (2 * j, 2 * j + 1):
            span = col(cum, h) + late[STEP + h : STEP + h + 1, :]
            m = pair * jnp.exp(jnp.where(past, span, -1e30))
            part.append(dot(m.astype(bf16), xb))
        inner.append(jnp.where(half, part[0], part[1]))

    wait_state(2)
    fades = [jnp.exp(fade_in[i][:1]) for i in range(n_groups - 1)]

    def carried(block):
        total = jnp.zeros((NSTATE, 256), f32)
        for i in range(n_groups - 2, -1, -1):
            fade = jnp.concatenate([both(fades[i], 2 * block + k) for k in range(2)], axis=1)
            total = jnp.where(group > i, total * fade + state_in[i, block].astype(f32), 0.0)
        return dot(read, total.astype(bf16))

    def send_back(third, tiles):
        send2[third] = packets(tiles)
        return_all(send2.at[third], recv2.at[third], two_send.at[third], two_recv.at[third])

    def results(block):
        rest = carried(block)
        return [
            inner[2 * block + k] + both(reach, 2 * block + k) * rest[:, 128 * k : 128 * (k + 1)]
            for k in range(2)
        ]

    wait_state(0)
    send_back(0, results(0))
    send_back(1, results(1))
    wait_state(1)
    send_back(2, results(2))

    loads[5].wait()
    lane = lanes(1)
    gated = []
    total = jnp.zeros((T, 1), f32)
    for third in range(3):
        wait_all(recv2.at[third], two_recv.at[third])
        block = recv2[third].astype(f32)
        for k in range(2):
            j = 2 * third + k
            cut = slice(128 * j, 128 * (j + 1))
            skip = jnp.where(lane < 64, skip_ref[2 * j], skip_ref[2 * j + 1])
            g = (unpack(block, k) + skip * value[:, cut]) * silu(gate[:, cut])
            total = total + jnp.sum(g * g, axis=-1, keepdims=True)
            gated.append(g * gain_ref[cut].reshape(1, 128))
    scale = lax.rsqrt(total * (1.0 / INNER) + 1e-5)
    normed = jnp.concatenate([g * scale for g in gated], axis=1).astype(bf16)
    normed = dot(frame_major(), normed).astype(bf16)
    loads[6].wait()
    o_ref[...] = (tok[...].astype(f32) + dot(normed, outw[...])).astype(bf16)

    for pair in halos:
        for (exists, _), copy in zip(toward, pair):
            pl.when(exists)(copy.wait_send)
    for i, buf in enumerate((send_e, send_a, send_b)):
        wait_all(buf, one_send.at[i])
    for part in range(3):
        for i, exists, other in later:
            pl.when(exists)(state_copy(part, i, other).wait_send)
    for third in range(3):
        wait_all(send2.at[third], two_send.at[third])


def per_device(
    n_tm,
    n_row,
    depth_tokens,
    mixer_weight,
    gate_weight,
    conv_kernel,
    conv_bias,
    step_bias,
    decay_rate,
    skip_gain,
    norm_gain,
    out_weight,
):
    hbm = pl.BlockSpec(memory_space=pltpu.HBM)
    vmem = pl.BlockSpec(memory_space=pltpu.VMEM)
    smem = pl.BlockSpec(memory_space=pltpu.SMEM)
    dma = pltpu.SemaphoreType.DMA
    n_groups = n_tm // GROUP
    out = pl.pallas_call(
        functools.partial(kernel, n_tm, n_row),
        out_shape=pltpu.VMEM((T, D), bf16),
        in_specs=[hbm] * 7 + [smem] * 3,
        out_specs=vmem,
        scratch_shapes=[
            pltpu.VMEM((T, D), bf16),
            pltpu.VMEM((2, T, D), bf16),
            pltpu.VMEM((CONV_CH, D), bf16),
            pltpu.VMEM((INNER + HEADS, D), bf16),
            pltpu.VMEM((INNER, D), bf16),
            pltpu.VMEM((3, 3, CONV_CH), f32),
            pltpu.VMEM((CONV_CH,), f32),
            pltpu.VMEM((INNER,), f32),
            pltpu.VMEM((T, D), bf16),
            pltpu.VMEM((T, CONV_CH), f32),
            pltpu.VMEM((2, T, CONV_CH), f32),
            pltpu.VMEM((T, INNER), f32),
            pltpu.VMEM((T, INNER), f32),
            pltpu.VMEM((GROUP, F // 2, 128), f32),
            pltpu.VMEM((GROUP, F // 2, 128), f32),
            pltpu.VMEM((GROUP, 4 * F, 128), bf16),
            pltpu.VMEM((GROUP, 4 * F, 128), bf16),
            pltpu.VMEM((GROUP, 2 * F, 128), bf16),
            pltpu.VMEM((GROUP, 2 * F, 128), bf16),
            pltpu.VMEM((3, NSTATE, 256), bf16),
            pltpu.VMEM((n_groups - 1, 3, NSTATE, 256), bf16),
            pltpu.VMEM((8, 128), f32),
            pltpu.VMEM((n_groups - 1, 8, 128), f32),
            pltpu.VMEM((3, GROUP, 2 * F, 128), bf16),
            pltpu.VMEM((3, GROUP, 2 * F, 128), bf16),
            pltpu.SemaphoreType.REGULAR((n_groups,)),
            dma((7,)),
            dma((2, WAVES)),
            dma((2, WAVES)),
            dma((3,)),
            dma((3,)),
            dma((3, n_groups - 1)),
            dma((3, n_groups - 1)),
            dma((3,)),
            dma((3,)),
        ],
        compiler_params=pltpu.CompilerParams(
            collective_id=0, has_side_effects=True, vmem_limit_bytes=56 * 1024 * 1024
        ),
    )(
        depth_tokens.reshape(T, D),
        mixer_weight.T,
        gate_weight.T,
        out_weight,
        conv_kernel,
        conv_bias,
        norm_gain,
        step_bias,
        decay_rate,
        skip_gain,
    )
    return out.reshape(depth_tokens.shape)


def solution(mesh):
    placed = (P("tm", "row", None, None), P(), P(), P(), P(), P(), P(), P(), P(), P())
    return jax.shard_map(
        functools.partial(per_device, mesh.shape["tm"], mesh.shape["row"]),
        mesh=mesh,
        in_specs=placed,
        out_specs=P("tm", "row", None, None),
        check_vma=False,
    )
```

```python
import functools

import jax
import jax.numpy as jnp
from jax import lax
from jax.experimental import pallas as pl
from jax.experimental.pallas import tpu as pltpu
from jax.sharding import PartitionSpec as P

D = 768
HEADS = 12
NSTATE = 16
GW = 16
INNER = 768
CONV_CH = 800
F = 8
T = F * GW
GROUP = 16
SPAN = 128
WAVES = 4
CELLS = GW // WAVES
ROWS = CELLS * F
PIECES = (0, 48, 80, 112, 128)
KEY = 0
STEP = 32

NT = ((1,), (1,))
TN = ((0,), (0,))
f32 = jnp.float32
bf16 = jnp.bfloat16


def lanes(rows):
    return lax.broadcasted_iota(jnp.int32, (rows, 128), 1)


def dot(a, b, dims=((1,), (0,)), precision=None):
    return lax.dot_general(a, b, (dims, ((), ())), preferred_element_type=f32, precision=precision)


def cell_major():
    r = lax.broadcasted_iota(jnp.int32, (T, T), 0)
    s = lax.broadcasted_iota(jnp.int32, (T, T), 1)
    return jnp.where(s == (r & (F - 1)) * GW + (r >> 3), 1.0, 0.0).astype(bf16)


def frame_major():
    r = lax.broadcasted_iota(jnp.int32, (T, T), 0)
    s = lax.broadcasted_iota(jnp.int32, (T, T), 1)
    return jnp.where(s == (r & (GW - 1)) * F + (r >> 4), 1.0, 0.0).astype(bf16)


def silu(x):
    return x / (1.0 + jnp.exp(-x))


def softplus(x):
    return jnp.maximum(x, 0.0) + jnp.log1p(jnp.exp(-jnp.abs(x)))


def convolve(wave, rows, taps, bias):
    low, high = ROWS * wave, ROWS * (wave + 1)

    def part(j, start, stop):
        z = [r(start, stop) for r in rows]
        return taps[0][j] * z[0] + taps[1][j] * z[1] + taps[2][j] * z[2]

    edge = jnp.zeros((F, bias.shape[1]), f32)
    if wave == 0:
        left = jnp.concatenate([edge, part(0, low, high - F)], axis=0)
    else:
        left = part(0, low - F, high - F)
    if wave == WAVES - 1:
        right = jnp.concatenate([part(2, low + F, high), edge], axis=0)
    else:
        right = part(2, low + F, high + F)
    return silu(part(1, low, high) + left + right + bias)


def packets(tiles):
    return jnp.concatenate([t.reshape(-1, F, 128) for t in tiles], axis=1).astype(bf16)


def unpack(block, j):
    return block[:, F * j : F * (j + 1)].reshape(SPAN, 128)


def kernel(
    n_tm,
    n_row,
    tok_hbm,
    mix_hbm,
    gate_hbm,
    out_hbm,
    taps_hbm,
    cbias_hbm,
    gain_hbm,
    sbias_ref,
    rate_ref,
    skip_ref,
    o_ref,
    tok,
    halo,
    mixw,
    gatew,
    outw,
    taps_ref,
    cbias_ref,
    gain_ref,
    mine,
    center,
    side,
    value,
    gate,
    send_e,
    recv_e,
    send_a,
    recv_a,
    send_b,
    recv_b,
    state_out,
    state_in,
    fade_out,
    fade_in,
    send2,
    recv2,
    ready,
    load_sem,
    halo_send,
    halo_recv,
    one_send,
    one_recv,
    state_send,
    state_recv,
    two_send,
    two_recv,
):
    me = lax.axis_index("tm")
    row = lax.axis_index("row")
    n_groups = n_tm // GROUP
    group = me // GROUP
    member = lax.rem(me, GROUP)
    cell = member
    my_wave, own_k = member // CELLS, lax.rem(member, CELLS)

    def peer(i):
        return lax.rem(member + i, GROUP)

    later = [(i, group + i < n_groups, me + GROUP * i) for i in range(1, n_groups)]
    earlier = [(i, group >= i, me - GROUP * i) for i in range(1, n_groups)]
    has_down, has_up = row > 0, row < n_row - 1
    toward = ((has_up, row + 1), (has_down, row - 1))
    origin = (has_down, has_up)

    loads = [
        pltpu.make_async_copy(src, dst, load_sem.at[i])
        for i, (src, dst) in enumerate(
            (
                (tok_hbm, tok),
                (gate_hbm, gatew),
                (mix_hbm, mixw),
                (taps_hbm, taps_ref),
                (cbias_hbm, cbias_ref),
                (gain_hbm, gain_ref),
                (out_hbm, outw),
            )
        )
    ]
    loads[0].start()

    barrier = pltpu.get_barrier_semaphore()
    for exists, other in toward:

        @pl.when(exists)
        def _():
            pl.semaphore_signal(barrier, inc=1, device_id={"row": other})

    def greet(i, c):
        pl.semaphore_signal(barrier, inc=1, device_id={"tm": group * GROUP + i})
        return c

    lax.fori_loop(member + 1, GROUP, greet, 0)
    for i, exists, other in later:

        @pl.when(exists)
        def _():
            pl.semaphore_signal(barrier, inc=1, device_id={"tm": other})

    for load in loads[1:]:
        load.start()
    perm = cell_major()
    loads[0].wait()
    own = dot(perm, tok[...]).astype(bf16)
    mine[...] = own
    neighbours = jnp.minimum(row, 1) + jnp.minimum(n_row - 1 - row, 1)
    pl.semaphore_wait(barrier, member + group + neighbours)

    pieces = [pl.ds(a, b - a) for a, b in zip(PIECES[:-1], PIECES[1:])]
    halos = [
        [
            pltpu.make_async_remote_copy(
                src_ref=mine.at[piece],
                dst_ref=halo.at[i, piece],
                send_sem=halo_send.at[i, w],
                recv_sem=halo_recv.at[i, w],
                device_id={"row": other},
            )
            for i, (_, other) in enumerate(toward)
        ]
        for w, piece in enumerate(pieces)
    ]
    for pair in halos:
        for (exists, _), copy in zip(toward, pair):
            pl.when(exists)(copy.start)

    def answer(i, c):
        pl.semaphore_signal(ready.at[member], inc=1, device_id={"tm": group * GROUP + i})
        return c

    lax.fori_loop(0, member, answer, 0)
    for i, exists, other in earlier:

        @pl.when(exists)
        def _():
            pl.semaphore_signal(ready.at[GROUP + i - 1], inc=1, device_id={"tm": other})

    loads[1].wait()
    gs = dot(own, gatew[...], NT).astype(bf16).astype(f32)
    gate[...] = gs[:, :INNER]
    steps = jnp.concatenate([gs[:, INNER:], jnp.zeros((T, 128 - HEADS), f32)], axis=1)
    steps = pltpu.roll(steps, STEP, 1)
    loads[2].wait()
    center[...] = dot(own, mixw[...], NT).astype(bf16).astype(f32)
    for load in loads[3:5]:
        load.wait()

    def activated(wave, sides, start, size):
        z = dot(sides, mixw[start : start + size, :], NT).astype(bf16).astype(f32)
        n = z.shape[0] // 2
        cols = slice(start, start + size)
        new = slice(PIECES[wave], PIECES[wave + 1])
        side[0, new, cols] = jnp.where(has_down, z[:n], 0.0)
        side[1, new, cols] = jnp.where(has_up, z[n:], 0.0)
        taps = [[taps_ref[i, j : j + 1, cols] for j in range(3)] for i in range(3)]
        rows = [
            lambda a, b: side[0, a:b, cols],
            lambda a, b: center[a:b, cols],
            lambda a, b: side[1, a:b, cols],
        ]
        return convolve(wave, rows, taps, cbias_ref[cols].reshape(1, size))

    def send_wave(wave, send, recv, which):
        def copy(k):
            other = CELLS * wave + k
            return pltpu.make_async_remote_copy(
                src_ref=send.at[other],
                dst_ref=recv.at[member],
                send_sem=one_send.at[which],
                recv_sem=one_recv.at[which],
                device_id={"tm": group * GROUP + other},
            )

        def one(k):
            if which == 0:
                other = CELLS * wave + k

                @pl.when(other > member)
                def _():
                    pl.semaphore_wait(ready.at[other], 1)

            copy(k).start()

        for i in range(1, CELLS):
            one(lax.rem(own_k + i, CELLS))

        @pl.when(my_wave == wave)
        def _():
            recv[member] = send[cell]

        @pl.when(my_wave != wave)
        def _():
            one(own_k)

    def return_all(send, recv, send_sem, recv_sem):
        for i in range(1, GROUP):
            other = peer(GROUP // 2 + (i // 2 if i % 2 else -(i // 2)))
            pltpu.make_async_remote_copy(
                src_ref=send.at[other],
                dst_ref=recv.at[cell],
                send_sem=send_sem,
                recv_sem=recv_sem,
                device_id={"tm": group * GROUP + other},
            ).start()
        recv[cell] = send[member]

    def wait_all(buf, sem, count=GROUP - 1):
        every = buf.at[pl.ds(0, count)]
        pltpu.make_async_copy(every, every, sem).wait()

    for wave in range(WAVES):
        for exists, copy in zip(origin, halos[wave]):
            pl.when(exists)(copy.wait_recv)
        rows = slice(ROWS * wave, ROWS * (wave + 1))
        cells = slice(CELLS * wave, CELLS * (wave + 1))
        sides = halo[:, PIECES[wave] : PIECES[wave + 1]].reshape(-1, D)
        key = activated(wave, sides, INNER, 32)
        key = jnp.concatenate([key, jnp.zeros((ROWS, 96), f32)], axis=1)
        extra = jnp.where(lanes(ROWS) < STEP, key, steps[rows])
        late = pltpu.roll(extra, 64, 1).reshape(CELLS, F, 128)[:, F // 2 :]
        early = extra.reshape(CELLS, F, 128)[:, : F // 2]
        front = lax.broadcasted_iota(jnp.int32, early.shape, 2) < 64
        send_e[cells] = jnp.where(front, early, late)
        send_wave(wave, send_e, recv_e, 0)
        act = activated(wave, sides, 0, 512)
        value[rows, :512] = act
        send_a[cells] = packets([act[:, 128 * j : 128 * (j + 1)] for j in range(4)])
        send_wave(wave, send_a, recv_a, 1)
        act = activated(wave, sides, 512, 256)
        value[rows, 512:] = act
        send_b[cells] = packets([act[:, 128 * j : 128 * (j + 1)] for j in range(2)])
        send_wave(wave, send_b, recv_b, 2)

    lane = lanes(1)
    bias_lane = jnp.zeros((1, 128), f32)
    rate_lane = jnp.zeros((1, 128), f32)
    for h in range(HEADS):
        bias_lane = jnp.where(lane == STEP + h, sbias_ref[h], bias_lane)
        rate_lane = jnp.where(lane == STEP + h, rate_ref[h], rate_lane)
    r = lax.broadcasted_iota(jnp.int32, (SPAN, SPAN), 0)
    s = lax.broadcasted_iota(jnp.int32, (SPAN, SPAN), 1)
    past = s <= r
    half = lanes(SPAN) < 64

    def col(a, h):
        return a[:, STEP + h : STEP + h + 1]

    def both(a, j):
        return jnp.where(half[: a.shape[0]], col(a, 2 * j), col(a, 2 * j + 1))

    blocks = (pl.ds(0, 2), pl.ds(2, 1))

    def state_copy(part, i, other):
        if part == 2:
            src, dst = fade_out, fade_in.at[i - 1]
        else:
            src, dst = state_out.at[blocks[part]], state_in.at[i - 1, blocks[part]]
        return pltpu.make_async_remote_copy(
            src_ref=src,
            dst_ref=dst,
            send_sem=state_send.at[part, i - 1],
            recv_sem=state_recv.at[part, i - 1],
            device_id={"tm": other},
        )

    def send_state(part):
        for i, exists, other in later:
            pl.when(exists)(state_copy(part, i, other).start)

    def wait_state(part):
        for i, exists, other in earlier:
            pl.when(exists)(state_copy(part, i, other).wait_recv)

    wait_all(recv_e, one_recv.at[0])
    early = recv_e[...]
    extra = jnp.concatenate([early, pltpu.roll(early, 64, 2)], axis=1).reshape(SPAN, 128)
    step = softplus(extra + bias_lane)
    tri = jnp.where(past, 1.0, 0.0).astype(f32)
    cum = dot(tri, -step * rate_lane, precision=lax.Precision.HIGHEST)
    end = cum[SPAN - 1 :, :]
    fade_out[...] = jnp.broadcast_to(end, (8, 128))
    for i, exists, other in later:

        @pl.when(exists)
        def _():
            pl.semaphore_wait(ready.at[GROUP + i - 1], 1)

    send_state(2)
    weight = jnp.exp(end - cum) * step
    write = extra[:, :NSTATE].astype(bf16)
    read = extra[:, NSTATE : 2 * NSTATE].astype(bf16)

    def local_state(j, x):
        scaled = jnp.concatenate([x[k] * both(weight, j + k) for k in range(2)], axis=1)
        state_out[j // 2] = dot(write, scaled.astype(bf16), TN).astype(bf16)

    wait_all(recv_a, one_recv.at[1])
    block = recv_a[...].astype(f32)
    x = [unpack(block, j) for j in range(4)]
    local_state(0, x[:2])
    local_state(2, x[2:])
    send_state(0)
    wait_all(recv_b, one_recv.at[2])
    block = recv_b[...].astype(f32)
    x = x + [unpack(block, j) for j in range(2)]
    local_state(4, x[4:])
    send_state(1)

    turned = jnp.transpose(jnp.where(half, cum, pltpu.roll(step, 64, 1)))
    reach = jnp.exp(cum)
    pair = dot(read, write, NT)
    inner = []
    for j in range(6):
        xb = x[j].astype(bf16)
        part = []
        for h in (2 * j, 2 * j + 1):
            at = STEP + h
            span = jnp.where(past, col(cum, h) - turned[at : at + 1, :], -1e30)
            m = pair * (jnp.exp(span) * turned[64 + at : 65 + at, :])
            part.append(dot(m.astype(bf16), xb))
        inner.append(jnp.where(half, part[0], part[1]))

    wait_state(2)
    fades = [jnp.exp(fade_in[i][:1]) for i in range(n_groups - 1)]

    def carried(block):
        total = jnp.zeros((NSTATE, 256), f32)
        for i in range(n_groups - 2, -1, -1):
            fade = jnp.concatenate([both(fades[i], 2 * block + k) for k in range(2)], axis=1)
            total = jnp.where(group > i, total * fade + state_in[i, block].astype(f32), 0.0)
        return dot(read, total.astype(bf16))

    def send_back(third, tiles):
        send2[third] = packets(tiles)
        return_all(send2.at[third], recv2.at[third], two_send.at[third], two_recv.at[third])

    def results(block):
        rest = carried(block)
        return [
            inner[2 * block + k] + both(reach, 2 * block + k) * rest[:, 128 * k : 128 * (k + 1)]
            for k in range(2)
        ]

    wait_state(0)
    send_back(0, results(0))
    send_back(1, results(1))
    wait_state(1)
    send_back(2, results(2))

    loads[5].wait()
    lane = lanes(1)
    gated = []
    total = jnp.zeros((T, 1), f32)
    for third in range(3):
        wait_all(recv2.at[third], two_recv.at[third])
        block = recv2[third].astype(f32)
        for k in range(2):
            j = 2 * third + k
            cut = slice(128 * j, 128 * (j + 1))
            skip = jnp.where(lane < 64, skip_ref[2 * j], skip_ref[2 * j + 1])
            g = (unpack(block, k) + skip * value[:, cut]) * silu(gate[:, cut])
            total = total + jnp.sum(g * g, axis=-1, keepdims=True)
            gated.append(g * gain_ref[cut].reshape(1, 128))
    scale = lax.rsqrt(total * (1.0 / INNER) + 1e-5)
    normed = jnp.concatenate([g * scale for g in gated], axis=1).astype(bf16)
    normed = dot(frame_major(), normed).astype(bf16)
    loads[6].wait()
    o_ref[...] = (tok[...].astype(f32) + dot(normed, outw[...])).astype(bf16)

    for pair in halos:
        for (exists, _), copy in zip(toward, pair):
            pl.when(exists)(copy.wait_send)
    for i, buf in enumerate((send_e, send_a, send_b)):
        wait_all(buf, one_send.at[i])
    for part in range(3):
        for i, exists, other in later:
            pl.when(exists)(state_copy(part, i, other).wait_send)
    for third in range(3):
        wait_all(send2.at[third], two_send.at[third])


def per_device(
    n_tm,
    n_row,
    depth_tokens,
    mixer_weight,
    gate_weight,
    conv_kernel,
    conv_bias,
    step_bias,
    decay_rate,
    skip_gain,
    norm_gain,
    out_weight,
):
    hbm = pl.BlockSpec(memory_space=pltpu.HBM)
    vmem = pl.BlockSpec(memory_space=pltpu.VMEM)
    smem = pl.BlockSpec(memory_space=pltpu.SMEM)
    dma = pltpu.SemaphoreType.DMA
    n_groups = n_tm // GROUP
    out = pl.pallas_call(
        functools.partial(kernel, n_tm, n_row),
        out_shape=pltpu.VMEM((T, D), bf16),
        in_specs=[hbm] * 7 + [smem] * 3,
        out_specs=vmem,
        scratch_shapes=[
            pltpu.VMEM((T, D), bf16),
            pltpu.VMEM((2, T, D), bf16),
            pltpu.VMEM((CONV_CH, D), bf16),
            pltpu.VMEM((INNER + HEADS, D), bf16),
            pltpu.VMEM((INNER, D), bf16),
            pltpu.VMEM((3, 3, CONV_CH), f32),
            pltpu.VMEM((CONV_CH,), f32),
            pltpu.VMEM((INNER,), f32),
            pltpu.VMEM((T, D), bf16),
            pltpu.VMEM((T, CONV_CH), f32),
            pltpu.VMEM((2, T, CONV_CH), f32),
            pltpu.VMEM((T, INNER), f32),
            pltpu.VMEM((T, INNER), f32),
            pltpu.VMEM((GROUP, F // 2, 128), f32),
            pltpu.VMEM((GROUP, F // 2, 128), f32),
            pltpu.VMEM((GROUP, 4 * F, 128), bf16),
            pltpu.VMEM((GROUP, 4 * F, 128), bf16),
            pltpu.VMEM((GROUP, 2 * F, 128), bf16),
            pltpu.VMEM((GROUP, 2 * F, 128), bf16),
            pltpu.VMEM((3, NSTATE, 256), bf16),
            pltpu.VMEM((n_groups - 1, 3, NSTATE, 256), bf16),
            pltpu.VMEM((8, 128), f32),
            pltpu.VMEM((n_groups - 1, 8, 128), f32),
            pltpu.VMEM((3, GROUP, 2 * F, 128), bf16),
            pltpu.VMEM((3, GROUP, 2 * F, 128), bf16),
            pltpu.SemaphoreType.REGULAR((GROUP + n_groups - 1,)),
            dma((7,)),
            dma((2, WAVES)),
            dma((2, WAVES)),
            dma((3,)),
            dma((3,)),
            dma((3, n_groups - 1)),
            dma((3, n_groups - 1)),
            dma((3,)),
            dma((3,)),
        ],
        compiler_params=pltpu.CompilerParams(
            collective_id=0, has_side_effects=True, vmem_limit_bytes=56 * 1024 * 1024
        ),
    )(
        depth_tokens.reshape(T, D),
        mixer_weight.T,
        gate_weight.T,
        out_weight,
        conv_kernel,
        conv_bias,
        norm_gain,
        step_bias,
        decay_rate,
        skip_gain,
    )
    return out.reshape(depth_tokens.shape)


def solution(mesh):
    placed = (P("tm", "row", None, None), P(), P(), P(), P(), P(), P(), P(), P(), P())
    return jax.shard_map(
        functools.partial(per_device, mesh.shape["tm"], mesh.shape["row"]),
        mesh=mesh,
        in_specs=placed,
        out_specs=P("tm", "row", None, None),
        check_vma=False,
    )
```

```python
import functools

import jax
import jax.numpy as jnp
from jax import lax
from jax.experimental import pallas as pl
from jax.experimental.pallas import tpu as pltpu
from jax.sharding import PartitionSpec as P

D = 768
HEADS = 12
NSTATE = 16
GW = 16
INNER = 768
CONV_CH = 800
F = 8
T = F * GW
GROUP = 16
SPAN = 128
WAVES = 4
CELLS = GW // WAVES
ROWS = CELLS * F
PIECES = (0, 48, 80, 112, 128)
KEY = 0
STEP = 32

NT = ((1,), (1,))
TN = ((0,), (0,))
f32 = jnp.float32
bf16 = jnp.bfloat16


def lanes(rows):
    return lax.broadcasted_iota(jnp.int32, (rows, 128), 1)


def dot(a, b, dims=((1,), (0,)), precision=None):
    return lax.dot_general(a, b, (dims, ((), ())), preferred_element_type=f32, precision=precision)


def cell_major():
    r = lax.broadcasted_iota(jnp.int32, (T, T), 0)
    s = lax.broadcasted_iota(jnp.int32, (T, T), 1)
    return jnp.where(s == (r & (F - 1)) * GW + (r >> 3), 1.0, 0.0).astype(bf16)


def frame_major():
    r = lax.broadcasted_iota(jnp.int32, (T, T), 0)
    s = lax.broadcasted_iota(jnp.int32, (T, T), 1)
    return jnp.where(s == (r & (GW - 1)) * F + (r >> 4), 1.0, 0.0).astype(bf16)


def silu(x):
    return x / (1.0 + jnp.exp(-x))


def softplus(x):
    return jnp.maximum(x, 0.0) + jnp.log1p(jnp.exp(-jnp.abs(x)))


def convolve(wave, rows, taps, bias):
    low, high = ROWS * wave, ROWS * (wave + 1)

    def part(j, start, stop):
        z = [r(start, stop) for r in rows]
        return taps[0][j] * z[0] + taps[1][j] * z[1] + taps[2][j] * z[2]

    edge = jnp.zeros((F, bias.shape[1]), f32)
    if wave == 0:
        left = jnp.concatenate([edge, part(0, low, high - F)], axis=0)
    else:
        left = part(0, low - F, high - F)
    if wave == WAVES - 1:
        right = jnp.concatenate([part(2, low + F, high), edge], axis=0)
    else:
        right = part(2, low + F, high + F)
    return silu(part(1, low, high) + left + right + bias)


def packets(tiles):
    return jnp.concatenate([t.reshape(-1, F, 128) for t in tiles], axis=1).astype(bf16)


def unpack(block, j):
    return block[:, F * j : F * (j + 1)].reshape(SPAN, 128)


def kernel(
    n_tm,
    n_row,
    tok_hbm,
    mix_hbm,
    gate_hbm,
    out_hbm,
    taps_hbm,
    cbias_hbm,
    gain_hbm,
    sbias_ref,
    rate_ref,
    skip_ref,
    o_ref,
    tok,
    halo,
    mixw,
    gatew,
    outw,
    taps_ref,
    cbias_ref,
    gain_ref,
    mine,
    center,
    side,
    value,
    gate,
    send_e,
    recv_e,
    send_a,
    recv_a,
    send_b,
    recv_b,
    state_out,
    state_in,
    fade_out,
    fade_in,
    send2,
    recv2,
    ready,
    load_sem,
    halo_send,
    halo_recv,
    one_send,
    one_recv,
    state_send,
    state_recv,
    two_send,
    two_recv,
):
    me = lax.axis_index("tm")
    row = lax.axis_index("row")
    n_groups = n_tm // GROUP
    group = me // GROUP
    member = lax.rem(me, GROUP)
    cell = member
    my_wave, own_k = member // CELLS, lax.rem(member, CELLS)

    def peer(i):
        return lax.rem(member + i, GROUP)

    later = [(i, group + i < n_groups, me + GROUP * i) for i in range(1, n_groups)]
    earlier = [(i, group >= i, me - GROUP * i) for i in range(1, n_groups)]
    has_down, has_up = row > 0, row < n_row - 1
    toward = ((has_up, row + 1), (has_down, row - 1))
    origin = (has_down, has_up)

    loads = [
        pltpu.make_async_copy(src, dst, load_sem.at[i])
        for i, (src, dst) in enumerate(
            (
                (tok_hbm, tok),
                (gate_hbm, gatew),
                (mix_hbm, mixw),
                (taps_hbm, taps_ref),
                (cbias_hbm, cbias_ref),
                (gain_hbm, gain_ref),
                (out_hbm, outw),
            )
        )
    ]
    loads[0].start()

    barrier = pltpu.get_barrier_semaphore()
    for exists, other in toward:

        @pl.when(exists)
        def _():
            pl.semaphore_signal(barrier, inc=1, device_id={"row": other})

    def greet(i, c):
        pl.semaphore_signal(barrier, inc=1, device_id={"tm": group * GROUP + i})
        return c

    lax.fori_loop(member + 1, GROUP, greet, 0)
    for i, exists, other in later:

        @pl.when(exists)
        def _():
            pl.semaphore_signal(barrier, inc=1, device_id={"tm": other})

    for load in loads[1:]:
        load.start()
    perm = cell_major()
    loads[0].wait()
    own = dot(perm, tok[...]).astype(bf16)
    mine[...] = own
    neighbours = jnp.minimum(row, 1) + jnp.minimum(n_row - 1 - row, 1)
    pl.semaphore_wait(barrier, member + group + neighbours)

    pieces = [pl.ds(a, b - a) for a, b in zip(PIECES[:-1], PIECES[1:])]
    halos = [
        [
            pltpu.make_async_remote_copy(
                src_ref=mine.at[piece],
                dst_ref=halo.at[i, piece],
                send_sem=halo_send.at[i, w],
                recv_sem=halo_recv.at[i, w],
                device_id={"row": other},
            )
            for i, (_, other) in enumerate(toward)
        ]
        for w, piece in enumerate(pieces)
    ]
    for pair in halos:
        for (exists, _), copy in zip(toward, pair):
            pl.when(exists)(copy.start)

    def answer(i, c):
        pl.semaphore_signal(ready.at[member], inc=1, device_id={"tm": group * GROUP + i})
        return c

    lax.fori_loop(0, member, answer, 0)
    for i, exists, other in earlier:

        @pl.when(exists)
        def _():
            pl.semaphore_signal(ready.at[GROUP + i - 1], inc=1, device_id={"tm": other})

    loads[1].wait()
    gs = dot(own, gatew[...], NT).astype(bf16).astype(f32)
    gate[...] = gs[:, :INNER]
    steps = jnp.concatenate([gs[:, INNER:], jnp.zeros((T, 128 - HEADS), f32)], axis=1)
    steps = pltpu.roll(steps, STEP, 1)
    loads[2].wait()
    center[...] = dot(own, mixw[...], NT).astype(bf16).astype(f32)
    for load in loads[3:5]:
        load.wait()

    def activated(wave, sides, start, size):
        z = dot(sides, mixw[start : start + size, :], NT).astype(bf16).astype(f32)
        n = z.shape[0] // 2
        cols = slice(start, start + size)
        new = slice(PIECES[wave], PIECES[wave + 1])
        side[0, new, cols] = jnp.where(has_down, z[:n], 0.0)
        side[1, new, cols] = jnp.where(has_up, z[n:], 0.0)
        taps = [[taps_ref[i, j : j + 1, cols] for j in range(3)] for i in range(3)]
        rows = [
            lambda a, b: side[0, a:b, cols],
            lambda a, b: center[a:b, cols],
            lambda a, b: side[1, a:b, cols],
        ]
        return convolve(wave, rows, taps, cbias_ref[cols].reshape(1, size))

    def send_wave(wave, send, recv, which):
        def copy(k):
            other = CELLS * wave + k
            return pltpu.make_async_remote_copy(
                src_ref=send.at[other],
                dst_ref=recv.at[member],
                send_sem=one_send.at[which],
                recv_sem=one_recv.at[which],
                device_id={"tm": group * GROUP + other},
            )

        def one(k):
            if which == 0:
                other = CELLS * wave + k

                @pl.when(other > member)
                def _():
                    pl.semaphore_wait(ready.at[other], 1)

            copy(k).start()

        for i in range(1, CELLS):
            one(lax.rem(own_k + i, CELLS))

        @pl.when(my_wave == wave)
        def _():
            recv[member] = send[cell]

        @pl.when(my_wave != wave)
        def _():
            one(own_k)

    def return_to(third, members):
        for other in members:

            @pl.when(other != member)
            def _():
                pltpu.make_async_remote_copy(
                    src_ref=send2.at[third, other],
                    dst_ref=recv2.at[third, cell],
                    send_sem=two_send.at[third],
                    recv_sem=two_recv.at[third],
                    device_id={"tm": group * GROUP + other},
                ).start()

    def wait_all(buf, sem, count=GROUP - 1):
        every = buf.at[pl.ds(0, count)]
        pltpu.make_async_copy(every, every, sem).wait()

    for wave in range(WAVES):
        for exists, copy in zip(origin, halos[wave]):
            pl.when(exists)(copy.wait_recv)
        rows = slice(ROWS * wave, ROWS * (wave + 1))
        cells = slice(CELLS * wave, CELLS * (wave + 1))
        sides = halo[:, PIECES[wave] : PIECES[wave + 1]].reshape(-1, D)
        key = activated(wave, sides, INNER, 32)
        key = jnp.concatenate([key, jnp.zeros((ROWS, 96), f32)], axis=1)
        extra = jnp.where(lanes(ROWS) < STEP, key, steps[rows])
        late = pltpu.roll(extra, 64, 1).reshape(CELLS, F, 128)[:, F // 2 :]
        early = extra.reshape(CELLS, F, 128)[:, : F // 2]
        front = lax.broadcasted_iota(jnp.int32, early.shape, 2) < 64
        send_e[cells] = jnp.where(front, early, late)
        send_wave(wave, send_e, recv_e, 0)
        act = activated(wave, sides, 0, 512)
        value[rows, :512] = act
        send_a[cells] = packets([act[:, 128 * j : 128 * (j + 1)] for j in range(4)])
        send_wave(wave, send_a, recv_a, 1)
        act = activated(wave, sides, 512, 256)
        value[rows, 512:] = act
        send_b[cells] = packets([act[:, 128 * j : 128 * (j + 1)] for j in range(2)])
        send_wave(wave, send_b, recv_b, 2)

    lane = lanes(1)
    bias_lane = jnp.zeros((1, 128), f32)
    rate_lane = jnp.zeros((1, 128), f32)
    for h in range(HEADS):
        bias_lane = jnp.where(lane == STEP + h, sbias_ref[h], bias_lane)
        rate_lane = jnp.where(lane == STEP + h, rate_ref[h], rate_lane)
    r = lax.broadcasted_iota(jnp.int32, (SPAN, SPAN), 0)
    s = lax.broadcasted_iota(jnp.int32, (SPAN, SPAN), 1)
    past = s <= r
    half = lanes(SPAN) < 64

    def col(a, h):
        return a[:, STEP + h : STEP + h + 1]

    def both(a, j):
        return jnp.where(half[: a.shape[0]], col(a, 2 * j), col(a, 2 * j + 1))

    blocks = (pl.ds(0, 2), pl.ds(2, 1))

    def state_copy(part, i, other):
        if part == 2:
            src, dst = fade_out, fade_in.at[i - 1]
        else:
            src, dst = state_out.at[blocks[part]], state_in.at[i - 1, blocks[part]]
        return pltpu.make_async_remote_copy(
            src_ref=src,
            dst_ref=dst,
            send_sem=state_send.at[part, i - 1],
            recv_sem=state_recv.at[part, i - 1],
            device_id={"tm": other},
        )

    def send_state(part):
        for i, exists, other in later:
            pl.when(exists)(state_copy(part, i, other).start)

    def wait_state(part):
        for i, exists, other in earlier:
            pl.when(exists)(state_copy(part, i, other).wait_recv)

    wait_all(recv_e, one_recv.at[0])
    early = recv_e[...]
    extra = jnp.concatenate([early, pltpu.roll(early, 64, 2)], axis=1).reshape(SPAN, 128)
    step = softplus(extra + bias_lane)
    tri = jnp.where(past, 1.0, 0.0).astype(f32)
    cum = dot(tri, -step * rate_lane, precision=lax.Precision.HIGHEST)
    end = cum[SPAN - 1 :, :]
    fade_out[...] = jnp.broadcast_to(end, (8, 128))
    for i, exists, other in later:

        @pl.when(exists)
        def _():
            pl.semaphore_wait(ready.at[GROUP + i - 1], 1)

    send_state(2)
    weight = jnp.exp(end - cum) * step
    write = extra[:, :NSTATE].astype(bf16)
    read = extra[:, NSTATE : 2 * NSTATE].astype(bf16)

    def local_state(j, x):
        scaled = jnp.concatenate([x[k] * both(weight, j + k) for k in range(2)], axis=1)
        state_out[j // 2] = dot(write, scaled.astype(bf16), TN).astype(bf16)

    wait_all(recv_a, one_recv.at[1])
    block = recv_a[...].astype(f32)
    x = [unpack(block, j) for j in range(4)]
    local_state(0, x[:2])
    local_state(2, x[2:])
    send_state(0)
    wait_all(recv_b, one_recv.at[2])
    block = recv_b[...].astype(f32)
    x = x + [unpack(block, j) for j in range(2)]
    local_state(4, x[4:])
    send_state(1)

    turned = jnp.transpose(jnp.where(half, cum, pltpu.roll(step, 64, 1)))
    reach = jnp.exp(cum)
    pair = dot(read, write, NT)
    inner = []
    for j in range(6):
        xb = x[j].astype(bf16)
        part = []
        for h in (2 * j, 2 * j + 1):
            at = STEP + h
            span = jnp.where(past, col(cum, h) - turned[at : at + 1, :], -1e30)
            m = pair * (jnp.exp(span) * turned[64 + at : 65 + at, :])
            part.append(dot(m.astype(bf16), xb))
        inner.append(jnp.where(half, part[0], part[1]))

    wait_state(2)
    fades = [jnp.exp(fade_in[i][:1]) for i in range(n_groups - 1)]

    def carried(block):
        total = jnp.zeros((NSTATE, 256), f32)
        for i in range(n_groups - 2, -1, -1):
            fade = jnp.concatenate([both(fades[i], 2 * block + k) for k in range(2)], axis=1)
            total = jnp.where(group > i, total * fade + state_in[i, block].astype(f32), 0.0)
        return dot(read, total.astype(bf16))

    def send_back(third, tiles):
        send2[third] = packets(tiles)
        return_to(third, range(GROUP // 4))
        recv2[third, cell] = send2[third, member]

    def results(block):
        rest = carried(block)
        return [
            inner[2 * block + k] + both(reach, 2 * block + k) * rest[:, 128 * k : 128 * (k + 1)]
            for k in range(2)
        ]

    wait_state(0)
    send_back(0, results(0))
    send_back(1, results(1))
    wait_state(1)
    send_back(2, results(2))
    for quarter in range(1, 4):
        for third in range(3):
            return_to(third, range(GROUP // 4 * quarter, GROUP // 4 * (quarter + 1)))

    loads[5].wait()
    lane = lanes(1)
    gated = []
    total = jnp.zeros((T, 1), f32)
    for third in range(3):
        wait_all(recv2.at[third], two_recv.at[third])
        block = recv2[third].astype(f32)
        for k in range(2):
            j = 2 * third + k
            cut = slice(128 * j, 128 * (j + 1))
            skip = jnp.where(lane < 64, skip_ref[2 * j], skip_ref[2 * j + 1])
            g = (unpack(block, k) + skip * value[:, cut]) * silu(gate[:, cut])
            total = total + jnp.sum(g * g, axis=-1, keepdims=True)
            gated.append(g * gain_ref[cut].reshape(1, 128))
    scale = lax.rsqrt(total * (1.0 / INNER) + 1e-5)
    normed = jnp.concatenate([g * scale for g in gated], axis=1).astype(bf16)
    normed = dot(frame_major(), normed).astype(bf16)
    loads[6].wait()
    o_ref[...] = (tok[...].astype(f32) + dot(normed, outw[...])).astype(bf16)

    for pair in halos:
        for (exists, _), copy in zip(toward, pair):
            pl.when(exists)(copy.wait_send)
    for i, buf in enumerate((send_e, send_a, send_b)):
        wait_all(buf, one_send.at[i])
    for part in range(3):
        for i, exists, other in later:
            pl.when(exists)(state_copy(part, i, other).wait_send)
    for third in range(3):
        wait_all(send2.at[third], two_send.at[third])


def per_device(
    n_tm,
    n_row,
    depth_tokens,
    mixer_weight,
    gate_weight,
    conv_kernel,
    conv_bias,
    step_bias,
    decay_rate,
    skip_gain,
    norm_gain,
    out_weight,
):
    hbm = pl.BlockSpec(memory_space=pltpu.HBM)
    vmem = pl.BlockSpec(memory_space=pltpu.VMEM)
    smem = pl.BlockSpec(memory_space=pltpu.SMEM)
    dma = pltpu.SemaphoreType.DMA
    n_groups = n_tm // GROUP
    out = pl.pallas_call(
        functools.partial(kernel, n_tm, n_row),
        out_shape=pltpu.VMEM((T, D), bf16),
        in_specs=[hbm] * 7 + [smem] * 3,
        out_specs=vmem,
        scratch_shapes=[
            pltpu.VMEM((T, D), bf16),
            pltpu.VMEM((2, T, D), bf16),
            pltpu.VMEM((CONV_CH, D), bf16),
            pltpu.VMEM((INNER + HEADS, D), bf16),
            pltpu.VMEM((INNER, D), bf16),
            pltpu.VMEM((3, 3, CONV_CH), f32),
            pltpu.VMEM((CONV_CH,), f32),
            pltpu.VMEM((INNER,), f32),
            pltpu.VMEM((T, D), bf16),
            pltpu.VMEM((T, CONV_CH), f32),
            pltpu.VMEM((2, T, CONV_CH), f32),
            pltpu.VMEM((T, INNER), f32),
            pltpu.VMEM((T, INNER), f32),
            pltpu.VMEM((GROUP, F // 2, 128), f32),
            pltpu.VMEM((GROUP, F // 2, 128), f32),
            pltpu.VMEM((GROUP, 4 * F, 128), bf16),
            pltpu.VMEM((GROUP, 4 * F, 128), bf16),
            pltpu.VMEM((GROUP, 2 * F, 128), bf16),
            pltpu.VMEM((GROUP, 2 * F, 128), bf16),
            pltpu.VMEM((3, NSTATE, 256), bf16),
            pltpu.VMEM((n_groups - 1, 3, NSTATE, 256), bf16),
            pltpu.VMEM((8, 128), f32),
            pltpu.VMEM((n_groups - 1, 8, 128), f32),
            pltpu.VMEM((3, GROUP, 2 * F, 128), bf16),
            pltpu.VMEM((3, GROUP, 2 * F, 128), bf16),
            pltpu.SemaphoreType.REGULAR((GROUP + n_groups - 1,)),
            dma((7,)),
            dma((2, WAVES)),
            dma((2, WAVES)),
            dma((3,)),
            dma((3,)),
            dma((3, n_groups - 1)),
            dma((3, n_groups - 1)),
            dma((3,)),
            dma((3,)),
        ],
        compiler_params=pltpu.CompilerParams(
            collective_id=0, has_side_effects=True, vmem_limit_bytes=56 * 1024 * 1024
        ),
    )(
        depth_tokens.reshape(T, D),
        mixer_weight.T,
        gate_weight.T,
        out_weight,
        conv_kernel,
        conv_bias,
        norm_gain,
        step_bias,
        decay_rate,
        skip_gain,
    )
    return out.reshape(depth_tokens.shape)


def solution(mesh):
    placed = (P("tm", "row", None, None), P(), P(), P(), P(), P(), P(), P(), P(), P())
    return jax.shard_map(
        functools.partial(per_device, mesh.shape["tm"], mesh.shape["row"]),
        mesh=mesh,
        in_specs=placed,
        out_specs=P("tm", "row", None, None),
        check_vma=False,
    )
```

```python
import functools

import jax
import jax.numpy as jnp
from jax import lax
from jax.experimental import pallas as pl
from jax.experimental.pallas import tpu as pltpu
from jax.sharding import PartitionSpec as P

D = 768
HEADS = 12
NSTATE = 16
GW = 16
INNER = 768
CONV_CH = 800
F = 8
T = F * GW
GROUP = 16
SPAN = 128
WAVES = 4
CELLS = GW // WAVES
ROWS = CELLS * F
PIECES = (0, 48, 80, 112, 128)
KEY = 0
STEP = 32

NT = ((1,), (1,))
TN = ((0,), (0,))
f32 = jnp.float32
bf16 = jnp.bfloat16


def lanes(rows):
    return lax.broadcasted_iota(jnp.int32, (rows, 128), 1)


def dot(a, b, dims=((1,), (0,)), precision=None):
    return lax.dot_general(a, b, (dims, ((), ())), preferred_element_type=f32, precision=precision)


def cell_major():
    r = lax.broadcasted_iota(jnp.int32, (T, T), 0)
    s = lax.broadcasted_iota(jnp.int32, (T, T), 1)
    return jnp.where(s == (r & (F - 1)) * GW + (r >> 3), 1.0, 0.0).astype(bf16)


def frame_major():
    r = lax.broadcasted_iota(jnp.int32, (T, T), 0)
    s = lax.broadcasted_iota(jnp.int32, (T, T), 1)
    return jnp.where(s == (r & (GW - 1)) * F + (r >> 4), 1.0, 0.0).astype(bf16)


def silu(x):
    return x / (1.0 + jnp.exp(-x))


def softplus(x):
    return jnp.maximum(x, 0.0) + jnp.log1p(jnp.exp(-jnp.abs(x)))


def convolve(wave, rows, taps, bias):
    low, high = ROWS * wave, ROWS * (wave + 1)

    def part(j, start, stop):
        z = [r(start, stop) for r in rows]
        return taps[0][j] * z[0] + taps[1][j] * z[1] + taps[2][j] * z[2]

    edge = jnp.zeros((F, bias.shape[1]), f32)
    if wave == 0:
        left = jnp.concatenate([edge, part(0, low, high - F)], axis=0)
    else:
        left = part(0, low - F, high - F)
    if wave == WAVES - 1:
        right = jnp.concatenate([part(2, low + F, high), edge], axis=0)
    else:
        right = part(2, low + F, high + F)
    return silu(part(1, low, high) + left + right + bias)


def packets(tiles):
    return jnp.concatenate([t.reshape(-1, F, 128) for t in tiles], axis=1).astype(bf16)


def unpack(block, j):
    return block[:, F * j : F * (j + 1)].reshape(SPAN, 128)


def kernel(
    n_tm,
    n_row,
    tok_hbm,
    mix_hbm,
    gate_hbm,
    out_hbm,
    taps_hbm,
    cbias_hbm,
    gain_hbm,
    sbias_ref,
    rate_ref,
    skip_ref,
    o_ref,
    tok,
    halo,
    mixw,
    gatew,
    outw,
    taps_ref,
    cbias_ref,
    gain_ref,
    mine,
    center,
    side,
    value,
    gate,
    send_e,
    recv_e,
    send_a,
    recv_a,
    send_b,
    recv_b,
    state_out,
    state_in,
    fade_out,
    fade_in,
    send2,
    recv2,
    ready,
    load_sem,
    halo_send,
    halo_recv,
    one_send,
    one_recv,
    state_send,
    state_recv,
    two_send,
    two_recv,
):
    me = lax.axis_index("tm")
    row = lax.axis_index("row")
    n_groups = n_tm // GROUP
    group = me // GROUP
    member = lax.rem(me, GROUP)
    cell = member
    my_wave, own_k = member // CELLS, lax.rem(member, CELLS)

    def peer(i):
        return lax.rem(member + i, GROUP)

    later = [(i, group + i < n_groups, me + GROUP * i) for i in range(1, n_groups)]
    earlier = [(i, group >= i, me - GROUP * i) for i in range(1, n_groups)]
    has_down, has_up = row > 0, row < n_row - 1
    toward = ((has_up, row + 1), (has_down, row - 1))
    origin = (has_down, has_up)

    loads = [
        pltpu.make_async_copy(src, dst, load_sem.at[i])
        for i, (src, dst) in enumerate(
            (
                (tok_hbm, tok),
                (gate_hbm, gatew),
                (mix_hbm, mixw),
                (taps_hbm, taps_ref),
                (cbias_hbm, cbias_ref),
                (gain_hbm, gain_ref),
                (out_hbm, outw),
            )
        )
    ]
    loads[0].start()

    barrier = pltpu.get_barrier_semaphore()
    for exists, other in toward:

        @pl.when(exists)
        def _():
            pl.semaphore_signal(barrier, inc=1, device_id={"row": other})

    def greet(i, c):
        pl.semaphore_signal(barrier, inc=1, device_id={"tm": group * GROUP + i})
        return c

    lax.fori_loop(member + 1, GROUP, greet, 0)
    for i, exists, other in later:

        @pl.when(exists)
        def _():
            pl.semaphore_signal(barrier, inc=1, device_id={"tm": other})

    for load in loads[1:]:
        load.start()
    perm = cell_major()
    loads[0].wait()
    own = dot(perm, tok[...]).astype(bf16)
    mine[...] = own
    neighbours = jnp.minimum(row, 1) + jnp.minimum(n_row - 1 - row, 1)
    pl.semaphore_wait(barrier, member + group + neighbours)

    pieces = [pl.ds(a, b - a) for a, b in zip(PIECES[:-1], PIECES[1:])]
    halos = [
        [
            pltpu.make_async_remote_copy(
                src_ref=mine.at[piece],
                dst_ref=halo.at[i, piece],
                send_sem=halo_send.at[i, w],
                recv_sem=halo_recv.at[i, w],
                device_id={"row": other},
            )
            for i, (_, other) in enumerate(toward)
        ]
        for w, piece in enumerate(pieces)
    ]
    for pair in halos:
        for (exists, _), copy in zip(toward, pair):
            pl.when(exists)(copy.start)

    def answer(i, c):
        pl.semaphore_signal(ready.at[member], inc=1, device_id={"tm": group * GROUP + i})
        return c

    lax.fori_loop(0, member, answer, 0)
    for i, exists, other in earlier:

        @pl.when(exists)
        def _():
            pl.semaphore_signal(ready.at[GROUP + i - 1], inc=1, device_id={"tm": other})

    loads[1].wait()
    gs = dot(own, gatew[...], NT).astype(bf16).astype(f32)
    gate[...] = gs[:, :INNER]
    steps = jnp.concatenate([gs[:, INNER:], jnp.zeros((T, 128 - HEADS), f32)], axis=1)
    steps = pltpu.roll(steps, STEP, 1)
    loads[2].wait()
    center[...] = dot(own, mixw[...], NT).astype(bf16).astype(f32)
    for load in loads[3:5]:
        load.wait()

    def activated(wave, sides, start, size):
        z = dot(sides, mixw[start : start + size, :], NT).astype(bf16).astype(f32)
        n = z.shape[0] // 2
        cols = slice(start, start + size)
        new = slice(PIECES[wave], PIECES[wave + 1])
        side[0, new, cols] = jnp.where(has_down, z[:n], 0.0)
        side[1, new, cols] = jnp.where(has_up, z[n:], 0.0)
        taps = [[taps_ref[i, j : j + 1, cols] for j in range(3)] for i in range(3)]
        rows = [
            lambda a, b: side[0, a:b, cols],
            lambda a, b: center[a:b, cols],
            lambda a, b: side[1, a:b, cols],
        ]
        return convolve(wave, rows, taps, cbias_ref[cols].reshape(1, size))

    def send_wave(wave, send, recv, which):
        def copy(k):
            other = CELLS * wave + k
            return pltpu.make_async_remote_copy(
                src_ref=send.at[other],
                dst_ref=recv.at[member],
                send_sem=one_send.at[which],
                recv_sem=one_recv.at[which],
                device_id={"tm": group * GROUP + other},
            )

        def one(k):
            if which == 0:
                other = CELLS * wave + k

                @pl.when(other > member)
                def _():
                    pl.semaphore_wait(ready.at[other], 1)

            copy(k).start()

        for i in range(1, CELLS):
            one(lax.rem(own_k + i, CELLS))

        @pl.when(my_wave == wave)
        def _():
            recv[member] = send[cell]

        @pl.when(my_wave != wave)
        def _():
            one(own_k)

    def return_to(third, members):
        for other in members:

            @pl.when(other != member)
            def _():
                pltpu.make_async_remote_copy(
                    src_ref=send2.at[third, other],
                    dst_ref=recv2.at[third, cell],
                    send_sem=two_send.at[third],
                    recv_sem=two_recv.at[third],
                    device_id={"tm": group * GROUP + other},
                ).start()

    def wait_all(buf, sem, count=GROUP - 1):
        every = buf.at[pl.ds(0, count)]
        pltpu.make_async_copy(every, every, sem).wait()

    for wave in range(WAVES):
        for exists, copy in zip(origin, halos[wave]):
            pl.when(exists)(copy.wait_recv)
        rows = slice(ROWS * wave, ROWS * (wave + 1))
        cells = slice(CELLS * wave, CELLS * (wave + 1))
        sides = halo[:, PIECES[wave] : PIECES[wave + 1]].reshape(-1, D)
        key = activated(wave, sides, INNER, 32)
        key = jnp.concatenate([key, jnp.zeros((ROWS, 96), f32)], axis=1)
        extra = jnp.where(lanes(ROWS) < STEP, key, steps[rows])
        late = pltpu.roll(extra, 64, 1).reshape(CELLS, F, 128)[:, F // 2 :]
        early = extra.reshape(CELLS, F, 128)[:, : F // 2]
        front = lax.broadcasted_iota(jnp.int32, early.shape, 2) < 64
        send_e[cells] = jnp.where(front, early, late)
        send_wave(wave, send_e, recv_e, 0)
        act = activated(wave, sides, 0, 512)
        value[rows, :512] = act
        send_a[cells] = packets([act[:, 128 * j : 128 * (j + 1)] for j in range(4)])
        send_wave(wave, send_a, recv_a, 1)
        act = activated(wave, sides, 512, 256)
        value[rows, 512:] = act
        send_b[cells] = packets([act[:, 128 * j : 128 * (j + 1)] for j in range(2)])
        send_wave(wave, send_b, recv_b, 2)

    lane = lanes(1)
    bias_lane = jnp.zeros((1, 128), f32)
    rate_lane = jnp.zeros((1, 128), f32)
    for h in range(HEADS):
        bias_lane = jnp.where(lane == STEP + h, sbias_ref[h], bias_lane)
        rate_lane = jnp.where(lane == STEP + h, rate_ref[h], rate_lane)
    r = lax.broadcasted_iota(jnp.int32, (SPAN, SPAN), 0)
    s = lax.broadcasted_iota(jnp.int32, (SPAN, SPAN), 1)
    past = s <= r
    half = lanes(SPAN) < 64

    def col(a, h):
        return a[:, STEP + h : STEP + h + 1]

    def both(a, j):
        return jnp.where(half[: a.shape[0]], col(a, 2 * j), col(a, 2 * j + 1))

    blocks = (pl.ds(0, 2), pl.ds(2, 1))

    def state_copy(part, i, other):
        if part == 2:
            src, dst = fade_out, fade_in.at[i - 1]
        else:
            src, dst = state_out.at[blocks[part]], state_in.at[i - 1, blocks[part]]
        return pltpu.make_async_remote_copy(
            src_ref=src,
            dst_ref=dst,
            send_sem=state_send.at[part, i - 1],
            recv_sem=state_recv.at[part, i - 1],
            device_id={"tm": other},
        )

    def send_state(part):
        for i, exists, other in later[1:] + later[:1]:
            pl.when(exists)(state_copy(part, i, other).start)

    def wait_state(part):
        for i, exists, other in earlier:
            pl.when(exists)(state_copy(part, i, other).wait_recv)

    wait_all(recv_e, one_recv.at[0])
    early = recv_e[...]
    extra = jnp.concatenate([early, pltpu.roll(early, 64, 2)], axis=1).reshape(SPAN, 128)
    step = softplus(extra + bias_lane)
    tri = jnp.where(past, 1.0, 0.0).astype(f32)
    cum = dot(tri, -step * rate_lane, precision=lax.Precision.HIGHEST)
    end = cum[SPAN - 1 :, :]
    fade_out[...] = jnp.broadcast_to(end, (8, 128))
    for i, exists, other in later:

        @pl.when(exists)
        def _():
            pl.semaphore_wait(ready.at[GROUP + i - 1], 1)

    send_state(2)
    weight = jnp.exp(end - cum) * step
    write = extra[:, :NSTATE].astype(bf16)
    read = extra[:, NSTATE : 2 * NSTATE].astype(bf16)

    def local_state(j, x):
        scaled = jnp.concatenate([x[k] * both(weight, j + k) for k in range(2)], axis=1)
        state_out[j // 2] = dot(write, scaled.astype(bf16), TN).astype(bf16)

    wait_all(recv_a, one_recv.at[1])
    block = recv_a[...].astype(f32)
    x = [unpack(block, j) for j in range(4)]
    local_state(0, x[:2])
    local_state(2, x[2:])
    send_state(0)
    wait_all(recv_b, one_recv.at[2])
    block = recv_b[...].astype(f32)
    x = x + [unpack(block, j) for j in range(2)]
    local_state(4, x[4:])
    send_state(1)

    turned = jnp.transpose(jnp.where(half, cum, pltpu.roll(step, 64, 1)))
    reach = jnp.exp(cum)
    pair = dot(read, write, NT)
    inner = []
    for j in range(6):
        xb = x[j].astype(bf16)
        part = []
        for h in (2 * j, 2 * j + 1):
            at = STEP + h
            span = jnp.where(past, col(cum, h) - turned[at : at + 1, :], -1e30)
            m = pair * (jnp.exp(span) * turned[64 + at : 65 + at, :])
            part.append(dot(m.astype(bf16), xb))
        inner.append(jnp.where(half, part[0], part[1]))

    wait_state(2)
    fades = [jnp.exp(fade_in[i][:1]) for i in range(n_groups - 1)]

    def carried(block):
        total = jnp.zeros((NSTATE, 256), f32)
        for i in range(n_groups - 2, -1, -1):
            fade = jnp.concatenate([both(fades[i], 2 * block + k) for k in range(2)], axis=1)
            total = jnp.where(group > i, total * fade + state_in[i, block].astype(f32), 0.0)
        return dot(read, total.astype(bf16))

    def send_back(third, tiles):
        send2[third] = packets(tiles)
        return_to(third, range(GROUP // 4))
        recv2[third, cell] = send2[third, member]

    def results(block):
        rest = carried(block)
        return [
            inner[2 * block + k] + both(reach, 2 * block + k) * rest[:, 128 * k : 128 * (k + 1)]
            for k in range(2)
        ]

    wait_state(0)
    send_back(0, results(0))
    send_back(1, results(1))
    wait_state(1)
    send_back(2, results(2))
    for quarter in range(1, 4):
        for third in range(3):
            return_to(third, range(GROUP // 4 * quarter, GROUP // 4 * (quarter + 1)))

    loads[5].wait()
    lane = lanes(1)
    gated = []
    total = jnp.zeros((T, 1), f32)
    for third in range(3):
        wait_all(recv2.at[third], two_recv.at[third])
        block = recv2[third].astype(f32)
        for k in range(2):
            j = 2 * third + k
            cut = slice(128 * j, 128 * (j + 1))
            skip = jnp.where(lane < 64, skip_ref[2 * j], skip_ref[2 * j + 1])
            g = (unpack(block, k) + skip * value[:, cut]) * silu(gate[:, cut])
            total = total + jnp.sum(g * g, axis=-1, keepdims=True)
            gated.append(g * gain_ref[cut].reshape(1, 128))
    scale = lax.rsqrt(total * (1.0 / INNER) + 1e-5)
    normed = jnp.concatenate([g * scale for g in gated], axis=1).astype(bf16)
    normed = dot(frame_major(), normed).astype(bf16)
    loads[6].wait()
    o_ref[...] = (tok[...].astype(f32) + dot(normed, outw[...])).astype(bf16)

    for pair in halos:
        for (exists, _), copy in zip(toward, pair):
            pl.when(exists)(copy.wait_send)
    for i, buf in enumerate((send_e, send_a, send_b)):
        wait_all(buf, one_send.at[i])
    for part in range(3):
        for i, exists, other in later:
            pl.when(exists)(state_copy(part, i, other).wait_send)
    for third in range(3):
        wait_all(send2.at[third], two_send.at[third])


def per_device(
    n_tm,
    n_row,
    depth_tokens,
    mixer_weight,
    gate_weight,
    conv_kernel,
    conv_bias,
    step_bias,
    decay_rate,
    skip_gain,
    norm_gain,
    out_weight,
):
    hbm = pl.BlockSpec(memory_space=pltpu.HBM)
    vmem = pl.BlockSpec(memory_space=pltpu.VMEM)
    smem = pl.BlockSpec(memory_space=pltpu.SMEM)
    dma = pltpu.SemaphoreType.DMA
    n_groups = n_tm // GROUP
    out = pl.pallas_call(
        functools.partial(kernel, n_tm, n_row),
        out_shape=pltpu.VMEM((T, D), bf16),
        in_specs=[hbm] * 7 + [smem] * 3,
        out_specs=vmem,
        scratch_shapes=[
            pltpu.VMEM((T, D), bf16),
            pltpu.VMEM((2, T, D), bf16),
            pltpu.VMEM((CONV_CH, D), bf16),
            pltpu.VMEM((INNER + HEADS, D), bf16),
            pltpu.VMEM((INNER, D), bf16),
            pltpu.VMEM((3, 3, CONV_CH), f32),
            pltpu.VMEM((CONV_CH,), f32),
            pltpu.VMEM((INNER,), f32),
            pltpu.VMEM((T, D), bf16),
            pltpu.VMEM((T, CONV_CH), f32),
            pltpu.VMEM((2, T, CONV_CH), f32),
            pltpu.VMEM((T, INNER), f32),
            pltpu.VMEM((T, INNER), f32),
            pltpu.VMEM((GROUP, F // 2, 128), f32),
            pltpu.VMEM((GROUP, F // 2, 128), f32),
            pltpu.VMEM((GROUP, 4 * F, 128), bf16),
            pltpu.VMEM((GROUP, 4 * F, 128), bf16),
            pltpu.VMEM((GROUP, 2 * F, 128), bf16),
            pltpu.VMEM((GROUP, 2 * F, 128), bf16),
            pltpu.VMEM((3, NSTATE, 256), bf16),
            pltpu.VMEM((n_groups - 1, 3, NSTATE, 256), bf16),
            pltpu.VMEM((8, 128), f32),
            pltpu.VMEM((n_groups - 1, 8, 128), f32),
            pltpu.VMEM((3, GROUP, 2 * F, 128), bf16),
            pltpu.VMEM((3, GROUP, 2 * F, 128), bf16),
            pltpu.SemaphoreType.REGULAR((GROUP + n_groups - 1,)),
            dma((7,)),
            dma((2, WAVES)),
            dma((2, WAVES)),
            dma((3,)),
            dma((3,)),
            dma((3, n_groups - 1)),
            dma((3, n_groups - 1)),
            dma((3,)),
            dma((3,)),
        ],
        compiler_params=pltpu.CompilerParams(
            collective_id=0, has_side_effects=True, vmem_limit_bytes=56 * 1024 * 1024
        ),
    )(
        depth_tokens.reshape(T, D),
        mixer_weight.T,
        gate_weight.T,
        out_weight,
        conv_kernel,
        conv_bias,
        norm_gain,
        step_bias,
        decay_rate,
        skip_gain,
    )
    return out.reshape(depth_tokens.shape)


def solution(mesh):
    placed = (P("tm", "row", None, None), P(), P(), P(), P(), P(), P(), P(), P(), P())
    return jax.shard_map(
        functools.partial(per_device, mesh.shape["tm"], mesh.shape["row"]),
        mesh=mesh,
        in_specs=placed,
        out_specs=P("tm", "row", None, None),
        check_vma=False,
    )
```
